256 devices in a mesh: chan: 64 (over y, z, x_lo), off: 4 (over x_hi, core).
Axes of the slice: x: 4 (x_hi: 2, x_lo: 2; x = x_hi * 2 + x_lo), y: 4, z: 8, core: 2. Of those that a mesh axis runs over, the one named last changes fastest.
Arguments:
- spectra: bfloat16 [16384, 128, 128], P('chan', 'off'), may hold values from -40 to 40
- pair_bins: int32 [64, 3, 256, 256], P('chan'), may hold values from 0 to 255, as said below
Outputs:
- stacked: float32 [256, 128], P(('chan', 'off'))
The draws below stay inside these ranges and needn't reach their ends.
Inputs may be any that keep to these rules, and one draw needn't show every extreme that they name: `pair_bins`: labels follow the fiber's geometry: a label is d * 4 + g, where d is a class of the distance along the fiber between the two channels and g the segment of the fiber that holds the second channel.
All inputs are finite; a program needn't handle non-finite values.
Results may differ from the reference program's by a relative error of at most 0.0003.
Values may be sent and summed in bfloat16 or wider, within the bound.
A program may use at most 128 MiB of HBM per device.

```python
import math
import jax
import jax.numpy as jnp
from jax import lax

CH = 256
F = 128
S = 64
SPAN = 2
BINS_DEV = 1
CHANNELS = 16384
N_CHAN = 64
N_OFF = 4


def draw_spectra(key, part):
    key = jax.random.fold_in(key, 11)
    noise_key, scale_key = jax.random.split(key)
    noise = jnp.clip(jax.random.normal(noise_key, (CHANNELS, F, 2 * S), jnp.float32), -4.0, 4.0)
    levels = jax.random.uniform(scale_key, (CHANNELS, F, S), jnp.float32, 0.0, jnp.log(10.0))
    scales = jnp.exp(levels)
    scales = jnp.concatenate([scales, scales], axis=-1)
    return (noise * scales).astype(jnp.bfloat16)


def draw_pair_bins(key, part):
    key = jax.random.fold_in(key, 23)
    gauge_key, coin_key = jax.random.split(key)
    gauge_level = jax.random.randint(gauge_key, (N_CHAN, 1), 0, 4, dtype=jnp.int32)
    coin_draws = jax.random.randint(coin_key, (N_CHAN, CH), 0, 4, dtype=jnp.int32)
    spacing = 1 + (coin_draws < gauge_level).astype(jnp.int32)
    spacing_line = spacing.reshape(-1)
    places = (jnp.cumsum(spacing_line) - spacing_line).reshape(N_CHAN, CH)
    loop_length = jnp.sum(spacing_line)
    blocks = jnp.arange(N_CHAN, dtype=jnp.int32)
    sections = N_OFF * BINS_DEV
    span_length = (SPAN + 1) * CH - 1
    channel_ids = jnp.arange(CH, dtype=jnp.int32)
    layers = []
    for step in range(SPAN + 1):
        partner = (blocks + step) % N_CHAN
        wrapped = jnp.where(blocks + step >= N_CHAN, loop_length, 0)
        far_places = places[partner] + wrapped[:, None]
        distance = jnp.abs(far_places[:, None, :] - places[:, :, None])
        offset_class = jnp.minimum(distance * N_CHAN // span_length, N_CHAN - 1)
        receiver = partner[:, None] * CH + channel_ids[None, :]
        segment = receiver * sections // CHANNELS
        layers.append(offset_class * sections + segment[:, None, :])
    return jnp.stack(layers, axis=1).astype(jnp.int32)


def setup_inputs(seed: int = 0) -> dict:
    keys = jax.random.split(jax.random.key(seed), 3)
    spectra = draw_spectra(jax.random.fold_in(keys[2], 71), 0)
    pair_bins = draw_pair_bins(jax.random.fold_in(keys[2], 71), 0)
    return dict(spectra=spectra, pair_bins=pair_bins)


def whiten(spectra):
    values = spectra.astype(jnp.float32)
    meansq = lax.optimization_barrier(jnp.mean(values * values, axis=-1, keepdims=True))
    return (values * lax.rsqrt(meansq + 1e-05)).astype(jnp.bfloat16)

def lag_table(freqs, nfreq, lags):
    shifts = jnp.arange(lags, dtype=jnp.int32) - lags // 2
    phase = jnp.mod(freqs[:, None] * shifts[None, :], 2 * nfreq)
    theta = math.pi * phase.astype(jnp.float32) / nfreq
    return jnp.concatenate([jnp.cos(theta), -jnp.sin(theta)], axis=0)

def cross_pairs(own, other):
    half = own.shape[-1] // 2
    rotated = jnp.concatenate([own[..., half:], -own[..., :half]], axis=-1)
    both = jnp.stack([own, rotated], axis=0).astype(jnp.float32)
    cross = jnp.einsum('rifs,jfs->rfij', both, other.astype(jnp.float32))
    cross = (cross * (1.0 / half)).astype(jnp.bfloat16)
    cross = lax.optimization_barrier(cross).astype(jnp.float32)
    return cross.reshape(2 * own.shape[1], own.shape[0], other.shape[0])

def reference(spectra, pair_bins):
    nbins = BINS_DEV * N_CHAN * N_OFF
    white = whiten(spectra)
    blocks = white.reshape(N_CHAN, CH, F, 2 * S)
    table = lag_table(jnp.arange(F, dtype=jnp.int32), F, F)

    def visit(carry, index):
        binned, counts = carry
        own = lax.dynamic_index_in_dim(blocks, index, 0, keepdims=False)
        for step in range(SPAN + 1):
            partner = ((index + step) % N_CHAN).astype(jnp.int32)
            other = lax.dynamic_index_in_dim(blocks, partner, 0, keepdims=False)
            cross = cross_pairs(own, other)
            flat = cross.reshape(2 * F, CH * CH).T
            labels = lax.dynamic_index_in_dim(pair_bins, index, 0, keepdims=False)[step].reshape(-1)
            binned = binned + jax.ops.segment_sum(flat, labels, num_segments=nbins)
            counts = counts + jax.ops.segment_sum(jnp.ones((CH * CH,), jnp.float32), labels, num_segments=nbins)
        return ((binned, counts), None)
    start = (jnp.zeros((nbins, 2 * F), jnp.float32), jnp.zeros((nbins,), jnp.float32))
    (binned, counts), _ = lax.scan(visit, start, jnp.arange(N_CHAN, dtype=jnp.int32))
    trace = jnp.dot(binned, table, precision=lax.Precision.HIGHEST, preferred_element_type=jnp.float32)
    return trace / jnp.sqrt(jnp.maximum(counts, 1.0))[:, None]
```

```python
import functools
import math

import jax
import jax.numpy as jnp
from jax import lax
from jax.experimental import pallas as pl
from jax.experimental.pallas import tpu as pltpu
from jax.sharding import PartitionSpec as P

F32 = jnp.float32
BF16 = jnp.bfloat16
MESH = pl.DeviceIdType.MESH
VMEM = pl.BlockSpec(memory_space=pltpu.VMEM)

CH = 256
LANES = 128
HALF = LANES // 2
SEGMENTS = 4
CLASSES = 64
PAD = 8
NEAR = 8
FAR = 32
FREQ_UNROLL = 8
ROW_UNROLL = 32


def whiten(raw, rows, white, with_rotated):
    freqs = raw.shape[1]
    step = freqs + PAD
    chunk = 32

    def normalise(block, _):
        values = raw[pl.ds(block * chunk, chunk)].astype(F32)
        meansq = jnp.mean(values * values, axis=-1, keepdims=True)
        scaled = values * lax.rsqrt(meansq + 1e-05)
        for channel in range(chunk):
            start = pl.multiple_of((block * chunk + channel) * step, 8)
            rows[pl.ds(start, freqs), :] = scaled[channel]
        return 0

    lax.fori_loop(0, CH // chunk, normalise, 0)

    def regroup(block, _):
        for part in range(FREQ_UNROLL):
            freq = block * FREQ_UNROLL + part
            values = rows[pl.ds(freq, CH, stride=step), :]
            white[freq, :CH, :] = values.astype(BF16)
            if with_rotated:
                lane = lax.broadcasted_iota(jnp.int32, (CH, LANES), 1)
                turned = pltpu.roll(values, HALF, 1)
                white[freq, CH:, :] = jnp.where(lane < HALF, turned, -turned).astype(BF16)
        return 0

    lax.fori_loop(0, freqs // FREQ_UNROLL, regroup, 0)


def cross_pairs(own, other, cross):
    freqs = other.shape[0]
    step = CH + PAD

    def body(block, _):
        for part in range(FREQ_UNROLL):
            freq = block * FREQ_UNROLL + part
            product = lax.dot_general(
                own[freq], other[freq], (((1,), (1,)), ((), ())), preferred_element_type=F32
            )
            for row in range(2):
                start = pl.multiple_of((freq + row * freqs) * step, 8)
                for side in range(2):
                    cross[side, pl.ds(start, CH), :] = product[
                        row * CH : (row + 1) * CH, side * LANES : (side + 1) * LANES
                    ]
        return 0

    lax.fori_loop(0, freqs // FREQ_UNROLL, body, 0)


def add_bins(cross, labels, slots, sums, counts):
    step = CH + PAD
    nrows = sums.shape[1]
    shape = (CLASSES // 16, 16, CH)
    slot_ids = lax.broadcasted_iota(jnp.int32, shape, 0) * 16 + lax.broadcasted_iota(jnp.int32, shape, 1)
    slot_ids = slot_ids.astype(F32).astype(BF16)
    one = jnp.ones((), BF16)
    zero = jnp.zeros((), BF16)
    segments = labels[...] & (SEGMENTS - 1)
    first, last = jnp.min(segments), jnp.max(segments)

    def add_segment(segment, _):
        marks = labels[...]
        classes = lax.shift_right_logical(marks, 2)
        slot = (classes & 1) * (CLASSES // 2) + lax.shift_right_logical(classes, 1)
        slots[...] = jnp.where((marks & (SEGMENTS - 1)) == segment, slot.astype(F32), -1.0)

        def add_rows(block, _):
            pieces, onehots = [], []
            tally = None
            for part in range(ROW_UNROLL):
                i = block * ROW_UNROLL + part
                sides = [cross[side, pl.ds(i, nrows, stride=step), :] for side in range(2)]
                pieces.append(jnp.concatenate(sides, axis=1).astype(BF16))
                row = jnp.broadcast_to(slots[pl.ds(i, 1), :], (16, CH)).astype(BF16)
                onehot = jnp.where(row[None] == slot_ids, one, zero).reshape(CLASSES, CH)
                onehots.append(onehot)
                tally = onehot if tally is None else tally + onehot
            sums[segment] += lax.dot_general(
                jnp.concatenate(pieces, axis=1),
                jnp.concatenate(onehots, axis=1),
                (((1,), (1,)), ((), ())),
                preferred_element_type=F32,
            )
            counts[segment] += tally.astype(F32)
            return 0

        lax.fori_loop(0, CH // ROW_UNROLL, add_rows, 0)
        return 0

    lax.fori_loop(first, last + 1, add_segment, 0)


def self_kernel(raw, labels, white, sums, counts, rows, cross, slots):
    sums[...] = jnp.zeros_like(sums)
    counts[...] = jnp.zeros_like(counts)
    whiten(raw, rows, white, True)
    cross_pairs(white, white.at[:, :CH, :], cross)
    add_bins(cross, labels, slots, sums, counts)


def pair_kernel(white, raw, labels, sums_in, counts_in, sums, counts, rows, other, cross, slots):
    sums[...] = sums_in[...]
    counts[...] = counts_in[...]
    whiten(raw, rows, other, False)
    cross_pairs(white, other, cross)
    add_bins(cross, labels, slots, sums, counts)


def last_kernel(
    white, raw, labels, sums_in, counts_in, table, share, parts, sums, counts, rows, other, cross, slots
):
    pair_kernel(white, raw, labels, sums_in, counts_in, sums, counts, rows, other, cross, slots)
    for segment in range(SEGMENTS):
        trace = lax.dot_general(
            sums[segment],
            table[...],
            (((0,), (0,)), ((), ())),
            precision=lax.Precision.HIGHEST,
            preferred_element_type=F32,
        )
        tally = jnp.sum(counts[segment], axis=1, keepdims=True) * share[0:1, :]
        for low in range(2):
            part = slice(low * FAR, (low + 1) * FAR)
            parts[segment * 2 + low, :, :LANES] = trace[part]
            parts[segment * 2 + low, :, LANES:] = tally[part]


def reduce_kernel(parts, out, near_in, far_out, far_in, near_send, near_recv, far_send, far_recv):
    chan, off = lax.axis_index("chan"), lax.axis_index("off")
    low, high = lax.rem(chan, 2), lax.div(chan, 2)
    near = off * 2 + low

    def near_device(step):
        index = lax.rem(near + step, NEAR)
        return index, (high * 2 + lax.rem(index, 2), lax.div(index, 2))

    def far_device(step):
        index = lax.rem(high + step, FAR)
        return index, (index * 2 + low, off)

    barrier = pltpu.get_barrier_semaphore()

    def greet_near(step, _):
        pl.semaphore_signal(barrier, inc=1, device_id=near_device(step)[1], device_id_type=MESH)
        return 0

    def greet_far(step, _):
        pl.semaphore_signal(barrier, inc=1, device_id=far_device(step)[1], device_id_type=MESH)
        return 0

    lax.fori_loop(1, FAR, greet_far, 0)
    lax.fori_loop(1, NEAR, greet_near, 0)
    pl.semaphore_wait(barrier, FAR - 1 + NEAR - 1)

    def near_copy(step):
        index, device = near_device(step)
        return pltpu.make_async_remote_copy(
            src_ref=parts.at[index],
            dst_ref=near_in.at[step - 1],
            send_sem=near_send.at[step - 1],
            recv_sem=near_recv.at[step - 1],
            device_id=device,
            device_id_type=MESH,
        )

    def far_copy(step):
        index, device = far_device(step)
        return pltpu.make_async_remote_copy(
            src_ref=far_out.at[index],
            dst_ref=far_in.at[step - 1],
            send_sem=far_send.at[step - 1],
            recv_sem=far_recv.at[step - 1],
            device_id=device,
            device_id_type=MESH,
        )

    def start_near(step, _):
        near_copy(step).start()
        return 0

    def start_far(step, _):
        far_copy(step).start()
        return 0

    lax.fori_loop(1, NEAR, start_near, 0)

    def add_near(step, total):
        near_copy(step).wait_recv()
        return total + near_in[step - 1]

    total = lax.fori_loop(1, NEAR, add_near, parts[near])
    for row in range(FAR):
        far_out[row] = total[row : row + 1]
    lax.fori_loop(1, FAR, start_far, 0)

    def add_far(step, total):
        far_copy(step).wait_recv()
        return total + far_in[step - 1]

    total = lax.fori_loop(1, FAR, add_far, far_out[high])
    out[...] = total[:, :LANES] / jnp.sqrt(jnp.maximum(total[:, LANES:], 1.0))

    def end_near(step, _):
        near_copy(step).wait_send()
        return 0

    def end_far(step, _):
        far_copy(step).wait_send()
        return 0

    lax.fori_loop(1, NEAR, end_near, 0)
    lax.fori_loop(1, FAR, end_far, 0)


def lag_table(freqs, nfreq, lags):
    shifts = jnp.arange(lags, dtype=jnp.int32) - lags // 2
    phase = jnp.mod(freqs[:, None] * shifts[None, :], 2 * nfreq)
    theta = math.pi * phase.astype(F32) / nfreq
    return jnp.concatenate([jnp.cos(theta), -jnp.sin(theta)], axis=0)


def from_ahead(value, steps):
    count = lax.axis_size("chan")
    pairs = [(source, (source - steps) % count) for source in range(count)]
    return lax.ppermute(value, "chan", pairs)


def on_device(spectra, pair_bins):
    freqs = spectra.shape[1]
    params = pltpu.CompilerParams(vmem_limit_bytes=48 * 1024 * 1024)
    rows = pltpu.VMEM((CH * (freqs + PAD), LANES), F32)
    other = pltpu.VMEM((freqs, CH, LANES), BF16)
    cross = pltpu.VMEM((2, 2 * freqs * (CH + PAD), LANES), F32)
    slots = pltpu.VMEM((CH, CH), F32)
    white_shape = jax.ShapeDtypeStruct((freqs, 2 * CH, LANES), BF16)
    sums_shape = jax.ShapeDtypeStruct((SEGMENTS, 2 * freqs, CLASSES), F32)
    counts_shape = jax.ShapeDtypeStruct((SEGMENTS, CLASSES, CH), F32)
    parts_shape = jax.ShapeDtypeStruct((NEAR, FAR, 2 * LANES), F32)

    ahead = [from_ahead(spectra, step) for step in (1, 2)]
    labels = pair_bins[0]
    nfreq = freqs * lax.axis_size("off")
    own_freqs = lax.axis_index("off") * freqs + jnp.arange(freqs, dtype=jnp.int32)
    table = lag_table(own_freqs, nfreq, LANES) * (1.0 / HALF)
    share = jnp.full((8, LANES), lax.axis_index("off") == 0, F32)

    white, sums, counts = pl.pallas_call(
        self_kernel,
        out_shape=[white_shape, sums_shape, counts_shape],
        in_specs=[VMEM] * 2,
        out_specs=[VMEM] * 3,
        scratch_shapes=[rows, cross, slots],
        compiler_params=params,
        cost_estimate=pl.CostEstimate(flops=3 * 10**9, bytes_accessed=10**7, transcendentals=0),
    )(spectra, labels[0])
    sums, counts = pl.pallas_call(
        pair_kernel,
        out_shape=[sums_shape, counts_shape],
        in_specs=[VMEM] * 5,
        out_specs=[VMEM] * 2,
        scratch_shapes=[rows, other, cross, slots],
        compiler_params=params,
        cost_estimate=pl.CostEstimate(flops=3 * 10**9, bytes_accessed=10**7, transcendentals=0),
    )(white, ahead[0], labels[1], sums, counts)
    parts = pl.pallas_call(
        last_kernel,
        out_shape=parts_shape,
        in_specs=[VMEM] * 7,
        out_specs=VMEM,
        scratch_shapes=[
            pltpu.VMEM(sums_shape.shape, F32),
            pltpu.VMEM(counts_shape.shape, F32),
            rows,
            other,
            cross,
            slots,
        ],
        compiler_params=params,
        cost_estimate=pl.CostEstimate(flops=3 * 10**9, bytes_accessed=10**7, transcendentals=0),
    )(white, ahead[1], labels[2], sums, counts, table, share)
    return pl.pallas_call(
        reduce_kernel,
        out_shape=jax.ShapeDtypeStruct((1, LANES), F32),
        in_specs=[VMEM],
        out_specs=VMEM,
        scratch_shapes=[
            pltpu.VMEM((NEAR - 1, FAR, 2 * LANES), F32),
            pltpu.VMEM((FAR, 1, 2 * LANES), F32),
            pltpu.VMEM((FAR - 1, 1, 2 * LANES), F32),
            pltpu.SemaphoreType.DMA((NEAR - 1,)),
            pltpu.SemaphoreType.DMA((NEAR - 1,)),
            pltpu.SemaphoreType.DMA((FAR - 1,)),
            pltpu.SemaphoreType.DMA((FAR - 1,)),
        ],
        compiler_params=pltpu.CompilerParams(collective_id=0, has_side_effects=True),
    )(parts)


def solution(mesh):
    in_specs = (P("chan", "off", None), P("chan", None, None, None))
    out_specs = P(("chan", "off"), None)
    return jax.shard_map(
        on_device, mesh=mesh, in_specs=in_specs, out_specs=out_specs, check_vma=False
    )
```

```python
import functools
import math

import jax
import jax.numpy as jnp
from jax import lax
from jax.experimental import pallas as pl
from jax.experimental.pallas import tpu as pltpu
from jax.sharding import PartitionSpec as P

F32 = jnp.float32
BF16 = jnp.bfloat16
MESH = pl.DeviceIdType.MESH
VMEM = pl.BlockSpec(memory_space=pltpu.VMEM)

CH = 256
LANES = 128
HALF = LANES // 2
SEGMENTS = 4
CLASSES = 64
PAD = 8
NEAR = 8
FAR = 32
FREQ_UNROLL = 8
ROW_UNROLL = 32


def whiten(raw, rows, white, with_rotated):
    freqs = raw.shape[1]
    step = freqs + PAD
    chunk = 32

    def normalise(block, _):
        values = raw[pl.ds(block * chunk, chunk)].astype(F32)
        meansq = jnp.mean(values * values, axis=-1, keepdims=True)
        scaled = values * lax.rsqrt(meansq + 1e-05)
        for channel in range(chunk):
            start = pl.multiple_of((block * chunk + channel) * step, 8)
            rows[pl.ds(start, freqs), :] = scaled[channel]
        return 0

    lax.fori_loop(0, CH // chunk, normalise, 0)

    def regroup(block, _):
        for part in range(FREQ_UNROLL):
            freq = block * FREQ_UNROLL + part
            values = rows[pl.ds(freq, CH, stride=step), :]
            white[freq, :CH, :] = values.astype(BF16)
            if with_rotated:
                lane = lax.broadcasted_iota(jnp.int32, (CH, LANES), 1)
                turned = pltpu.roll(values, HALF, 1)
                white[freq, CH:, :] = jnp.where(lane < HALF, turned, -turned).astype(BF16)
        return 0

    lax.fori_loop(0, freqs // FREQ_UNROLL, regroup, 0)


def cross_pairs(first, second, cross, top):
    freqs = second.shape[0]
    step = CH + PAD

    def body(block, _):
        for part in range(FREQ_UNROLL):
            freq = block * FREQ_UNROLL + part
            product = lax.dot_general(
                first[freq], second[freq, :CH, :], (((1,), (1,)), ((), ())), preferred_element_type=F32
            )
            for row in range(2):
                start = pl.multiple_of((top + freq + row * freqs) * step, 8)
                for side in range(2):
                    cross[side, pl.ds(start, CH), :] = product[
                        row * CH : (row + 1) * CH, side * LANES : (side + 1) * LANES
                    ]
        return 0

    lax.fori_loop(0, freqs // FREQ_UNROLL, body, 0)


def add_bins(cross, read_labels, weight, slots, nrows, add_sums, counts):
    step = CH + PAD
    shape = (CLASSES // 16, 16, CH)
    slot_ids = lax.broadcasted_iota(jnp.int32, shape, 0) * 16 + lax.broadcasted_iota(jnp.int32, shape, 1)
    slot_ids = slot_ids.astype(F32).astype(BF16)
    one = jnp.ones((), BF16)
    zero = jnp.zeros((), BF16)
    segments = read_labels() & (SEGMENTS - 1)
    first, last = jnp.min(segments), jnp.max(segments)

    def add_segment(segment, _):
        marks = read_labels()
        classes = lax.shift_right_logical(marks, 2)
        slot = (classes & 1) * (CLASSES // 2) + lax.shift_right_logical(classes, 1)
        slots[...] = jnp.where((marks & (SEGMENTS - 1)) == segment, slot.astype(F32), -1.0)

        def add_rows(block, _):
            pieces, onehots = [], []
            tally = None
            for part in range(ROW_UNROLL):
                i = block * ROW_UNROLL + part
                sides = [cross[side, pl.ds(i, nrows, stride=step), :] for side in range(2)]
                pieces.append(jnp.concatenate(sides, axis=1).astype(BF16))
                row = jnp.broadcast_to(slots[pl.ds(i, 1), :], (16, CH)).astype(BF16)
                onehot = jnp.where(row[None] == slot_ids, one, zero).reshape(CLASSES, CH)
                onehots.append(onehot)
                tally = onehot if tally is None else tally + onehot
            add_sums(
                segment,
                lax.dot_general(
                    jnp.concatenate(pieces, axis=1),
                    jnp.concatenate(onehots, axis=1),
                    (((1,), (1,)), ((), ())),
                    preferred_element_type=F32,
                ),
            )
            counts[segment] += tally.astype(F32) * weight
            return 0

        lax.fori_loop(0, CH // ROW_UNROLL, add_rows, 0)
        return 0

    lax.fori_loop(first, last + 1, add_segment, 0)


def self_kernel(raw, labels, white, sums, counts, rows, cross, slots):
    sums[...] = jnp.zeros_like(sums)
    counts[...] = jnp.zeros_like(counts)
    half = white.shape[1]
    whiten(raw, rows, white.reshape(2 * half, 2 * CH, LANES), True)
    for side in range(2):
        cross_pairs(white.at[side], white.at[side], cross, side * 2 * half)

    def add_sums(segment, values):
        for side in range(2):
            sums[segment, side] += values[side * 2 * half : (side + 1) * 2 * half]

    weight = (lax.axis_index("off") == 0).astype(F32)
    add_bins(cross, lambda: labels[...], weight, slots, 4 * half, add_sums, counts)


def pairs_kernel(
    own, beside, after, before, labels, labels_beside, labels_before, sums_in, counts_in, table,
    parts, sums, counts, white, rows, cross, slots, own_sem,
):
    half = own.shape[1]
    copy = pltpu.make_async_copy(own, white.at[0:2], own_sem)
    copy.start()
    sums[...] = sums_in[...]
    counts[...] = counts_in[...]
    whiten(beside, rows, white.at[2], True)
    whiten(after, rows, white.at[3], False)
    whiten(before, rows, white.at[4], True)
    copy.wait()
    low = lax.rem(lax.axis_index("chan"), 2)
    counted = (lax.axis_index("off") == 0).astype(F32)
    even = (1 - low).astype(F32) * counted
    odd = low.astype(F32) * counted

    def moved(ref):
        return ref[...].astype(F32).astype(jnp.int32)

    def choose(if_even, if_odd):
        return lambda: jnp.where(low == 0, if_even(), if_odd())

    own_near, own_far = lambda: labels[1], lambda: labels[2]
    beside_near = lambda: moved(labels_beside)
    before_near, before_far = lambda: moved(labels_before.at[0]), lambda: moved(labels_before.at[1])
    jobs = (
        ((0, 2), (2, 1), choose(own_near, beside_near), low, even),
        ((0, 3), (4, 1), choose(own_far, before_far), low, even),
        ((2, 3), (4, 2), choose(beside_near, before_near), low, even),
        ((4, 1), (0, 3), choose(before_far, own_far), 1 - low, odd),
    )
    for if_even, if_odd, read_labels, side, weight in jobs:
        first = if_even[0] + low * (if_odd[0] - if_even[0])
        second = if_even[1] + low * (if_odd[1] - if_even[1])
        cross_pairs(white.at[first], white.at[second], cross, 0)

        def add_sums(segment, values):
            sums[segment, side] += values

        add_bins(cross, read_labels, weight, slots, 2 * half, add_sums, counts)
    for segment in range(SEGMENTS):
        trace = lax.dot_general(
            sums[segment].reshape(4 * half, CLASSES),
            table[...],
            (((0,), (0,)), ((), ())),
            precision=lax.Precision.HIGHEST,
            preferred_element_type=F32,
        )
        tally = jnp.sum(counts[segment], axis=1, keepdims=True)
        for part in range(2):
            piece = slice(part * FAR, (part + 1) * FAR)
            parts[segment * 2 + part, :, :LANES] = trace[piece]
            parts[segment * 2 + part, :, LANES:] = jnp.broadcast_to(tally[piece], (FAR, LANES))


def reduce_kernel(parts, out, near_in, far_out, far_in, near_send, near_recv, far_send, far_recv):
    chan, off = lax.axis_index("chan"), lax.axis_index("off")
    low, high = lax.rem(chan, 2), lax.div(chan, 2)
    near = off * 2 + low

    def near_device(step):
        index = lax.rem(near + step, NEAR)
        return index, (high * 2 + lax.rem(index, 2), lax.div(index, 2))

    def far_device(step):
        index = lax.rem(high + step, FAR)
        return index, (index * 2 + low, off)

    barrier = pltpu.get_barrier_semaphore()

    def greet_near(step, _):
        pl.semaphore_signal(barrier, inc=1, device_id=near_device(step)[1], device_id_type=MESH)
        return 0

    def greet_far(step, _):
        pl.semaphore_signal(barrier, inc=1, device_id=far_device(step)[1], device_id_type=MESH)
        return 0

    lax.fori_loop(1, FAR, greet_far, 0)
    lax.fori_loop(1, NEAR, greet_near, 0)
    pl.semaphore_wait(barrier, FAR - 1 + NEAR - 1)

    def near_copy(step):
        index, device = near_device(step)
        return pltpu.make_async_remote_copy(
            src_ref=parts.at[index],
            dst_ref=near_in.at[step - 1],
            send_sem=near_send.at[step - 1],
            recv_sem=near_recv.at[step - 1],
            device_id=device,
            device_id_type=MESH,
        )

    def far_copy(step):
        index, device = far_device(step)
        return pltpu.make_async_remote_copy(
            src_ref=far_out.at[index],
            dst_ref=far_in.at[step - 1],
            send_sem=far_send.at[step - 1],
            recv_sem=far_recv.at[step - 1],
            device_id=device,
            device_id_type=MESH,
        )

    def start_near(step, _):
        near_copy(step).start()
        return 0

    def start_far(step, _):
        far_copy(step).start()
        return 0

    lax.fori_loop(1, NEAR, start_near, 0)

    def add_near(step, total):
        near_copy(step).wait_recv()
        return total + near_in[step - 1]

    total = lax.fori_loop(1, NEAR, add_near, parts[near])
    for row in range(FAR):
        far_out[row] = total[row : row + 1]
    lax.fori_loop(1, FAR, start_far, 0)

    def add_far(step, total):
        far_copy(step).wait_recv()
        return total + far_in[step - 1]

    total = lax.fori_loop(1, FAR, add_far, far_out[high])
    out[...] = total[:, :LANES] / jnp.sqrt(jnp.maximum(total[:, LANES:], 1.0))

    def end_near(step, _):
        near_copy(step).wait_send()
        return 0

    def end_far(step, _):
        far_copy(step).wait_send()
        return 0

    lax.fori_loop(1, NEAR, end_near, 0)
    lax.fori_loop(1, FAR, end_far, 0)


def lag_table(freqs, nfreq, lags):
    shifts = jnp.arange(lags, dtype=jnp.int32) - lags // 2
    phase = jnp.mod(freqs[:, None] * shifts[None, :], 2 * nfreq)
    theta = math.pi * phase.astype(F32) / nfreq
    return jnp.stack([jnp.cos(theta), -jnp.sin(theta)], axis=0)


def shifted(value, steps):
    count = lax.axis_size("chan")
    return lax.ppermute(value, "chan", [(place, (place + steps) % count) for place in range(count)])


def swapped(value):
    count = lax.axis_size("chan")
    return lax.ppermute(value, "chan", [(place, place ^ 1) for place in range(count)])


def on_device(spectra, pair_bins):
    freqs = spectra.shape[1]
    half = freqs // 2
    low = lax.rem(lax.axis_index("chan"), 2)
    params = pltpu.CompilerParams(vmem_limit_bytes=48 * 1024 * 1024)
    sums_shape = jax.ShapeDtypeStruct((SEGMENTS, 2, 2 * half, CLASSES), F32)
    counts_shape = jax.ShapeDtypeStruct((SEGMENTS, CLASSES, CH), F32)
    slots = pltpu.VMEM((CH, CH), F32)
    cost = pl.CostEstimate(flops=3 * 10**9, bytes_accessed=10**7, transcendentals=0)

    labels = pair_bins[0]
    after = shifted(spectra[:, :half], -2)
    before = shifted(spectra[:, half:], 2)
    beside = swapped(lax.dynamic_slice_in_dim(spectra, (1 - low) * half, half, 1))
    sent_labels = labels[1:].astype(BF16)
    labels_beside = swapped(sent_labels[0])
    labels_before = shifted(sent_labels, 2)

    nfreq = freqs * lax.axis_size("off")
    own_freqs = lax.axis_index("off") * freqs + jnp.arange(freqs, dtype=jnp.int32)
    table = lag_table(own_freqs, nfreq, LANES) * (1.0 / HALF)
    table = table.reshape(2, 2, half, LANES).swapaxes(0, 1).reshape(2 * freqs, LANES)

    white, sums, counts = pl.pallas_call(
        self_kernel,
        out_shape=[jax.ShapeDtypeStruct((2, half, 2 * CH, LANES), BF16), sums_shape, counts_shape],
        in_specs=[VMEM] * 2,
        out_specs=[VMEM] * 3,
        scratch_shapes=[
            pltpu.VMEM((CH * (freqs + PAD), LANES), F32),
            pltpu.VMEM((2, 2 * freqs * (CH + PAD), LANES), F32),
            slots,
        ],
        compiler_params=params,
        cost_estimate=cost,
    )(spectra, labels[0])
    parts = pl.pallas_call(
        pairs_kernel,
        out_shape=jax.ShapeDtypeStruct((NEAR, FAR, 2 * LANES), F32),
        in_specs=[pl.BlockSpec(memory_space=pl.ANY)] + [VMEM] * 9,
        out_specs=VMEM,
        scratch_shapes=[
            pltpu.VMEM(sums_shape.shape, F32),
            pltpu.VMEM(counts_shape.shape, F32),
            pltpu.VMEM((5, half, 2 * CH, LANES), BF16),
            pltpu.VMEM((CH * (half + PAD), LANES), F32),
            pltpu.VMEM((2, 2 * half * (CH + PAD), LANES), F32),
            slots,
            pltpu.SemaphoreType.DMA,
        ],
        compiler_params=params,
        cost_estimate=cost,
    )(white, beside, after, before, labels, labels_beside, labels_before, sums, counts, table)
    return pl.pallas_call(
        reduce_kernel,
        out_shape=jax.ShapeDtypeStruct((1, LANES), F32),
        in_specs=[VMEM],
        out_specs=VMEM,
        scratch_shapes=[
            pltpu.VMEM((NEAR - 1, FAR, 2 * LANES), F32),
            pltpu.VMEM((FAR, 1, 2 * LANES), F32),
            pltpu.VMEM((FAR - 1, 1, 2 * LANES), F32),
            pltpu.SemaphoreType.DMA((NEAR - 1,)),
            pltpu.SemaphoreType.DMA((NEAR - 1,)),
            pltpu.SemaphoreType.DMA((FAR - 1,)),
            pltpu.SemaphoreType.DMA((FAR - 1,)),
        ],
        compiler_params=pltpu.CompilerParams(collective_id=0, has_side_effects=True),
    )(parts)


def solution(mesh):
    in_specs = (P("chan", "off", None), P("chan", None, None, None))
    out_specs = P(("chan", "off"), None)
    return jax.shard_map(
        on_device, mesh=mesh, in_specs=in_specs, out_specs=out_specs, check_vma=False
    )
```

```python
import functools
import math

import jax
import jax.numpy as jnp
import numpy as np
from jax import lax
from jax.experimental import pallas as pl
from jax.experimental.pallas import tpu as pltpu
from jax.sharding import PartitionSpec as P

F32 = jnp.float32
BF16 = jnp.bfloat16
MESH = pl.DeviceIdType.MESH
VMEM = pl.BlockSpec(memory_space=pltpu.VMEM)
ANY = pl.BlockSpec(memory_space=pl.ANY)
DMA = pltpu.SemaphoreType.DMA

CH = 256
LANES = 128
HALF = LANES // 2
SEGMENTS = 4
CLASSES = 64
PAD = 8
NEAR = 8
FAR = 32
FREQ_UNROLL = 8
ROW_UNROLL = 64
SELF_UNROLL = 32
COUNT_ROWS = 8


def whiten(raw, rows, white, with_rotated):
    freqs = raw.shape[1]
    step = freqs + PAD
    chunk = 32

    def normalise(block, _):
        values = raw[pl.ds(block * chunk, chunk)].astype(F32)
        meansq = jnp.mean(values * values, axis=-1, keepdims=True)
        scaled = values * lax.rsqrt(meansq + 1e-05)
        for channel in range(chunk):
            start = pl.multiple_of((block * chunk + channel) * step, 8)
            rows[pl.ds(start, freqs), :] = scaled[channel]
        return 0

    lax.fori_loop(0, CH // chunk, normalise, 0)

    def regroup(block, _):
        for part in range(FREQ_UNROLL):
            freq = block * FREQ_UNROLL + part
            values = rows[pl.ds(freq, CH, stride=step), :]
            white[freq, :CH, :] = values.astype(BF16)
            if with_rotated:
                lane = lax.broadcasted_iota(jnp.int32, (CH, LANES), 1)
                turned = pltpu.roll(values, HALF, 1)
                white[freq, CH:, :] = jnp.where(lane < HALF, turned, -turned).astype(BF16)
        return 0

    lax.fori_loop(0, freqs // FREQ_UNROLL, regroup, 0)


def cross_pairs(first, second, cross, top):
    freqs = second.shape[0]
    step = CH + PAD

    def body(block, _):
        for part in range(FREQ_UNROLL):
            freq = block * FREQ_UNROLL + part
            product = lax.dot_general(
                first[freq], second[freq, :CH, :], (((1,), (1,)), ((), ())), preferred_element_type=F32
            )
            for row in range(2):
                start = pl.multiple_of((top + freq + row * freqs) * step, 8)
                for side in range(2):
                    cross[side, pl.ds(start, CH), :] = product[
                        row * CH : (row + 1) * CH, side * LANES : (side + 1) * LANES
                    ]
        return 0

    lax.fori_loop(0, freqs // FREQ_UNROLL, body, 0)


def add_bins(cross, read_labels, weight, slots, nrows, add_sums, counts):
    step = CH + PAD
    slot_ids = slot_numbers()
    one = jnp.ones((), BF16)
    zero = jnp.zeros((), BF16)
    segments = read_labels() & (SEGMENTS - 1)
    first, last = jnp.min(segments), jnp.max(segments)

    def add_segment(segment, _):
        marks = read_labels()
        slots[...] = jnp.where((marks & (SEGMENTS - 1)) == segment, slots_of(marks), -1.0)

        def add_rows(block, _):
            pieces, onehots = [], []
            tally = None
            for part in range(ROW_UNROLL):
                i = block * ROW_UNROLL + part
                sides = [cross[side, pl.ds(i, nrows, stride=step), :] for side in range(2)]
                pieces.append(jnp.concatenate(sides, axis=1).astype(BF16))
                row = jnp.broadcast_to(slots[pl.ds(i, 1), :], (16, CH)).astype(BF16)
                onehot = jnp.where(row[None] == slot_ids, one, zero).reshape(CLASSES, CH)
                onehots.append(onehot)
                tally = onehot if tally is None else tally + onehot
            add_sums(
                segment,
                lax.dot_general(
                    jnp.concatenate(pieces, axis=1),
                    jnp.concatenate(onehots, axis=1),
                    (((1,), (1,)), ((), ())),
                    preferred_element_type=F32,
                ),
            )
            counts[segment] += tally.astype(F32) * weight
            return 0

        lax.fori_loop(0, CH // ROW_UNROLL, add_rows, 0)
        return 0

    lax.fori_loop(first, last + 1, add_segment, 0)


def slot_numbers():
    shape = (CLASSES // 16, 16, CH)
    ids = lax.broadcasted_iota(jnp.int32, shape, 0) * 16 + lax.broadcasted_iota(jnp.int32, shape, 1)
    return ids.astype(F32).astype(BF16)


def slots_of(marks):
    classes = lax.shift_right_logical(marks, 2)
    return ((classes & 1) * (CLASSES // 2) + lax.shift_right_logical(classes, 1)).astype(F32)


def add_all_bins(cross, slots, segments, nrows, sums, tally):
    step = CH + PAD
    slot_ids = slot_numbers()
    row_ids = lax.broadcasted_iota(jnp.int32, (16, CH), 0).astype(F32).astype(BF16)
    one = jnp.ones((), BF16)
    zero = jnp.zeros((), BF16)

    def add_rows(block, _):
        pieces, onehots = [], []
        for part in range(SELF_UNROLL):
            i = block * SELF_UNROLL + part
            sides = [cross[side, pl.ds(i, nrows, stride=step), :] for side in range(2)]
            values = jnp.concatenate(sides, axis=1).astype(BF16).reshape(nrows // 16, 16, CH)
            place = jnp.broadcast_to(segments[pl.ds(i, 1), :], (16, CH)).astype(BF16)
            masked = [
                jnp.where(place[None] == jnp.full((), segment, BF16), values, zero).reshape(nrows, CH)
                for segment in range(SEGMENTS)
            ]
            masked.append(jnp.where(place == row_ids, one, zero))
            pieces.append(jnp.concatenate(masked, axis=0))
            row = jnp.broadcast_to(slots[pl.ds(i, 1), :], (16, CH)).astype(BF16)
            onehots.append(jnp.where(row[None] == slot_ids, one, zero).reshape(CLASSES, CH))
        binned = lax.dot_general(
            jnp.concatenate(pieces, axis=1),
            jnp.concatenate(onehots, axis=1),
            (((1,), (1,)), ((), ())),
            preferred_element_type=F32,
        )
        for segment in range(SEGMENTS):
            sums[segment] += binned[segment * nrows : (segment + 1) * nrows].reshape(sums.shape[1:])
        tally[...] += binned[SEGMENTS * nrows :]
        return 0

    lax.fori_loop(0, CH // SELF_UNROLL, add_rows, 0)


def exchange_kernel(
    spectra, pair_bins, after, before, beside, labels_before, labels_beside, white_out, sums, tally,
    raw, labels, sent_labels, white, rows, cross, slots, segments, local_sem, send_sem, recv_sem,
):
    half = white.shape[1]
    chan, off = lax.axis_index("chan"), lax.axis_index("off")
    count = lax.axis_size("chan")
    low = lax.rem(chan, 2)
    down, up = lax.rem(chan + count - 2, count), lax.rem(chan + 2, count)
    partner = chan + 1 - 2 * low
    load_raw = pltpu.make_async_copy(spectra, raw, local_sem.at[0])
    load_labels = pltpu.make_async_copy(pair_bins.at[0], labels, local_sem.at[1])
    load_labels.start()
    load_raw.start()
    barrier = pltpu.get_barrier_semaphore()
    for neighbour in (partner, down, up):
        pl.semaphore_signal(barrier, inc=1, device_id=(neighbour, off), device_id_type=MESH)
    pl.semaphore_wait(barrier, 3)

    def send(index, source, target, chan_to):
        copy = pltpu.make_async_remote_copy(
            src_ref=source,
            dst_ref=target,
            send_sem=send_sem.at[index],
            recv_sem=recv_sem.at[index],
            device_id=(chan_to, off),
            device_id_type=MESH,
        )
        copy.start()
        return copy

    other_half = pl.ds(pl.multiple_of((1 - low) * half, half), half)
    copies = [
        send(0, spectra.at[:, half : 2 * half, :], before, up),
        send(1, spectra.at[:, 0:half, :], after, down),
        send(2, spectra.at[:, other_half, :], beside, partner),
    ]
    load_labels.wait()
    sent_labels[...] = labels[1:].astype(F32).astype(BF16)
    copies.append(send(3, sent_labels, labels_before, up))
    copies.append(send(4, sent_labels.at[0], labels_beside, partner))
    marks = labels[0]
    slots[...] = slots_of(marks)
    segments[...] = (marks & (SEGMENTS - 1)).astype(F32)
    sums[...] = jnp.zeros_like(sums)
    tally[...] = jnp.zeros_like(tally)
    load_raw.wait()
    whiten(raw, rows, white.reshape(2 * half, 2 * CH, LANES), True)
    keep = pltpu.make_async_copy(white, white_out, local_sem.at[2])
    keep.start()
    for side in range(2):
        cross_pairs(white.at[side], white.at[side], cross, side * 2 * half)
    add_all_bins(cross, slots, segments, 4 * half, sums, tally)
    keep.wait()
    for copy in copies:
        copy.wait()


def pairs_kernel(
    own, beside, after, before, labels, labels_beside, labels_before, sums_in,
    sums, counts, white, raw, rows, cross, slots, load_sem,
):
    half = own.shape[1]
    loads = [
        pltpu.make_async_copy(block, raw.at[index], load_sem.at[index])
        for index, block in enumerate((beside, after, before))
    ]
    load_own = pltpu.make_async_copy(own, white.at[0:2], load_sem.at[3])
    for load in loads:
        load.start()
    load_own.start()
    sums[...] = sums_in[...]
    counts[...] = jnp.zeros_like(counts)
    for index, load in enumerate(loads):
        load.wait()
        whiten(raw.at[index], rows, white.at[2 + index], index != 1)
    load_own.wait()
    low = lax.rem(lax.axis_index("chan"), 2)
    counted = (lax.axis_index("off") == 0).astype(F32)
    even = (1 - low).astype(F32) * counted
    odd = low.astype(F32) * counted

    def moved(ref):
        return ref[...].astype(F32).astype(jnp.int32)

    def choose(if_even, if_odd):
        return lambda: jnp.where(low == 0, if_even(), if_odd())

    own_near, own_far = lambda: labels[1], lambda: labels[2]
    beside_near = lambda: moved(labels_beside)
    before_near, before_far = lambda: moved(labels_before.at[0]), lambda: moved(labels_before.at[1])
    jobs = (
        ((0, 2), (2, 1), choose(own_near, beside_near), low, even),
        ((0, 3), (4, 1), choose(own_far, before_far), low, even),
        ((2, 3), (4, 2), choose(beside_near, before_near), low, even),
        ((4, 1), (0, 3), choose(before_far, own_far), 1 - low, odd),
    )
    for if_even, if_odd, read_labels, side, weight in jobs:
        first = if_even[0] + low * (if_odd[0] - if_even[0])
        second = if_even[1] + low * (if_odd[1] - if_even[1])
        cross_pairs(white.at[first], white.at[second], cross, 0)

        def add_sums(segment, values):
            sums[segment, side] += values

        add_bins(cross, read_labels, weight, slots, 2 * half, add_sums, counts)


def reduce_kernel(
    sums, counts, self_tally, table, out, parts, near_in, far_out, far_in, near_send, near_recv, far_send, far_recv
):
    chan, off = lax.axis_index("chan"), lax.axis_index("off")
    low, high = lax.rem(chan, 2), lax.div(chan, 2)
    near = off * 2 + low

    def near_device(step):
        index = lax.rem(near + step, NEAR)
        return index, (high * 2 + lax.rem(index, 2), lax.div(index, 2))

    def far_device(step):
        index = lax.rem(high + step, FAR)
        return index, (index * 2 + low, off)

    barrier = pltpu.get_barrier_semaphore()

    def greet_near(step, _):
        pl.semaphore_signal(barrier, inc=1, device_id=near_device(step)[1], device_id_type=MESH)
        return 0

    def greet_far(step, _):
        pl.semaphore_signal(barrier, inc=1, device_id=far_device(step)[1], device_id_type=MESH)
        return 0

    lax.fori_loop(1, NEAR, greet_near, 0)
    lax.fori_loop(1, FAR, greet_far, 0)
    ones = jnp.ones((COUNT_ROWS, CH), F32)
    for segment in range(SEGMENTS):
        trace = lax.dot_general(
            sums[segment].reshape(table.shape[1], CLASSES),
            table[off],
            (((0,), (0,)), ((), ())),
            precision=lax.Precision.HIGHEST,
            preferred_element_type=F32,
        )
        tally = lax.dot_general(
            ones,
            counts[segment],
            (((1,), (1,)), ((), ())),
            precision=lax.Precision.HIGHEST,
            preferred_element_type=F32,
        )
        own = self_tally[segment : segment + 1, :] * (off == 0).astype(F32)
        tally = tally + jnp.broadcast_to(own, tally.shape)
        tally = jnp.concatenate([tally, jnp.zeros((COUNT_ROWS, LANES - CLASSES), F32)], axis=1)
        for part in range(2):
            parts[segment * 2 + part, :FAR, :] = trace[part * FAR : (part + 1) * FAR]
            parts[segment * 2 + part, FAR:, :] = tally
    pl.semaphore_wait(barrier, FAR - 1 + NEAR - 1)

    def near_copy(step):
        index, device = near_device(step)
        return pltpu.make_async_remote_copy(
            src_ref=parts.at[index],
            dst_ref=near_in.at[step - 1],
            send_sem=near_send.at[step - 1],
            recv_sem=near_recv.at[step - 1],
            device_id=device,
            device_id_type=MESH,
        )

    def far_copy(step):
        index, device = far_device(step)
        return pltpu.make_async_remote_copy(
            src_ref=far_out.at[index],
            dst_ref=far_in.at[step - 1],
            send_sem=far_send.at[step - 1],
            recv_sem=far_recv.at[step - 1],
            device_id=device,
            device_id_type=MESH,
        )

    def start_near(step, _):
        near_copy(step).start()
        return 0

    def start_far(step, _):
        far_copy(step).start()
        return 0

    lax.fori_loop(1, NEAR, start_near, 0)

    def add_near(step, total):
        near_copy(step).wait_recv()
        return total + near_in[step - 1]

    total = lax.fori_loop(1, NEAR, add_near, parts[near])
    for row in range(FAR):
        far_out[row] = jnp.concatenate([total[row : row + 1], total[FAR : FAR + 1]], axis=1)
    lax.fori_loop(1, FAR, start_far, 0)

    def add_far(step, total):
        far_copy(step).wait_recv()
        return total + far_in[step - 1]

    total = lax.fori_loop(1, FAR, add_far, far_out[high])
    lane = lax.broadcasted_iota(jnp.int32, (1, LANES), 1)
    count = jnp.sum(jnp.where(lane == low * FAR + high, total[:, LANES:], 0.0), axis=1, keepdims=True)
    out[...] = total[:, :LANES] / jnp.sqrt(jnp.maximum(count, 1.0))

    def end_near(step, _):
        near_copy(step).wait_send()
        return 0

    def end_far(step, _):
        far_copy(step).wait_send()
        return 0

    lax.fori_loop(1, NEAR, end_near, 0)
    lax.fori_loop(1, FAR, end_far, 0)


def lag_tables(groups, freqs, lags):
    nfreq = groups * freqs
    shifts = np.arange(lags) - lags // 2
    theta = math.pi * np.mod(np.arange(nfreq)[:, None] * shifts[None, :], 2 * nfreq) / nfreq
    table = np.stack([np.cos(theta), -np.sin(theta)]).reshape(2, groups, 2, freqs // 2, lags)
    table = table.transpose(1, 2, 0, 3, 4).reshape(groups, 2 * freqs, lags)
    return jnp.asarray((table / HALF).astype(np.float32))


def on_device(spectra, pair_bins):
    freqs = spectra.shape[1]
    half = freqs // 2
    vmem_limit = 56 * 1024 * 1024
    white_shape = jax.ShapeDtypeStruct((2, half, 2 * CH, LANES), BF16)
    block_shape = jax.ShapeDtypeStruct((CH, half, LANES), BF16)
    sums_shape = jax.ShapeDtypeStruct((SEGMENTS, 2, 2 * half, CLASSES), F32)
    counts_shape = jax.ShapeDtypeStruct((SEGMENTS, CLASSES, CH), F32)
    square = pltpu.VMEM((CH, CH), F32)

    after, before, beside, labels_before, labels_beside, white, sums, tally = pl.pallas_call(
        exchange_kernel,
        out_shape=[
            block_shape,
            block_shape,
            block_shape,
            jax.ShapeDtypeStruct((2, CH, CH), BF16),
            jax.ShapeDtypeStruct((CH, CH), BF16),
            white_shape,
            sums_shape,
            jax.ShapeDtypeStruct((16, CLASSES), F32),
        ],
        in_specs=[ANY] * 2,
        out_specs=[ANY] * 6 + [VMEM] * 2,
        scratch_shapes=[
            pltpu.VMEM(spectra.shape, BF16),
            pltpu.VMEM(pair_bins.shape[1:], jnp.int32),
            pltpu.VMEM((2, CH, CH), BF16),
            pltpu.VMEM(white_shape.shape, BF16),
            pltpu.VMEM((CH * (freqs + PAD), LANES), F32),
            pltpu.VMEM((2, 2 * freqs * (CH + PAD), LANES), F32),
            square,
            square,
            DMA((3,)),
            DMA((5,)),
            DMA((5,)),
        ],
        compiler_params=pltpu.CompilerParams(
            collective_id=1, has_side_effects=True, vmem_limit_bytes=vmem_limit
        ),
    )(spectra, pair_bins)
    sums, counts = pl.pallas_call(
        pairs_kernel,
        out_shape=[sums_shape, counts_shape],
        in_specs=[ANY] * 4 + [VMEM] * 4,
        out_specs=[VMEM] * 2,
        scratch_shapes=[
            pltpu.VMEM((5, half, 2 * CH, LANES), BF16),
            pltpu.VMEM((3, CH, half, LANES), BF16),
            pltpu.VMEM((CH * (half + PAD), LANES), F32),
            pltpu.VMEM((2, 2 * half * (CH + PAD), LANES), F32),
            square,
            DMA((4,)),
        ],
        compiler_params=pltpu.CompilerParams(vmem_limit_bytes=vmem_limit),
    )(white, beside, after, before, pair_bins[0], labels_beside, labels_before, sums)
    return pl.pallas_call(
        reduce_kernel,
        out_shape=jax.ShapeDtypeStruct((1, LANES), F32),
        in_specs=[VMEM] * 4,
        out_specs=VMEM,
        scratch_shapes=[
            pltpu.VMEM((NEAR, FAR + COUNT_ROWS, LANES), F32),
            pltpu.VMEM((NEAR - 1, FAR + COUNT_ROWS, LANES), F32),
            pltpu.VMEM((FAR, 1, 2 * LANES), F32),
            pltpu.VMEM((FAR - 1, 1, 2 * LANES), F32),
            DMA((NEAR - 1,)),
            DMA((NEAR - 1,)),
            DMA((FAR - 1,)),
            DMA((FAR - 1,)),
        ],
        compiler_params=pltpu.CompilerParams(collective_id=0, has_side_effects=True),
    )(sums, counts, tally, lag_tables(lax.axis_size("off"), freqs, LANES))


def solution(mesh):
    in_specs = (P("chan", "off", None), P("chan", None, None, None))
    out_specs = P(("chan", "off"), None)
    return jax.shard_map(
        on_device, mesh=mesh, in_specs=in_specs, out_specs=out_specs, check_vma=False
    )
```

```python
import functools
import math

import jax
import jax.numpy as jnp
import numpy as np
from jax import lax
from jax.experimental import pallas as pl
from jax.experimental.pallas import tpu as pltpu
from jax.sharding import PartitionSpec as P

F32 = jnp.float32
BF16 = jnp.bfloat16
MESH = pl.DeviceIdType.MESH
VMEM = pl.BlockSpec(memory_space=pltpu.VMEM)
ANY = pl.BlockSpec(memory_space=pl.ANY)
DMA = pltpu.SemaphoreType.DMA

CH = 256
LANES = 128
EARLY = CH // 2
HALF = LANES // 2
SEGMENTS = 4
CLASSES = 64
PAD = 8
NEAR = 8
FAR = 32
FREQ_UNROLL = 8
ROW_UNROLL = 64
SELF_UNROLL = 32
COUNT_ROWS = 8


def whiten(raw, rows, white, with_rotated):
    channels, freqs, _ = raw.shape
    step = freqs + PAD
    chunk = 32

    def normalise(block, _):
        values = raw[pl.ds(block * chunk, chunk)].astype(F32)
        meansq = jnp.mean(values * values, axis=-1, keepdims=True)
        scaled = values * lax.rsqrt(meansq + 1e-05)
        for channel in range(chunk):
            start = pl.multiple_of((block * chunk + channel) * step, 8)
            rows[pl.ds(start, freqs), :] = scaled[channel]
        return 0

    lax.fori_loop(0, channels // chunk, normalise, 0)

    def regroup(block, _):
        for part in range(FREQ_UNROLL):
            freq = block * FREQ_UNROLL + part
            values = rows[pl.ds(freq, channels, stride=step), :]
            white[freq, 0] = values.astype(BF16)
            if with_rotated:
                lane = lax.broadcasted_iota(jnp.int32, (channels, LANES), 1)
                turned = pltpu.roll(values, HALF, 1)
                white[freq, 1] = jnp.where(lane < HALF, turned, -turned).astype(BF16)
        return 0

    lax.fori_loop(0, freqs // FREQ_UNROLL, regroup, 0)


def cross_pairs(first, second, cross, freqs, top=0):
    step = CH + PAD

    def body(block, _):
        for part in range(FREQ_UNROLL):
            freq = block * FREQ_UNROLL + part
            product = lax.dot_general(
                first(freq), second(freq), (((1,), (1,)), ((), ())), preferred_element_type=F32
            )
            for row in range(2):
                start = pl.multiple_of((top + freq + row * freqs) * step, 8)
                for side in range(product.shape[1] // LANES):
                    cross[side, pl.ds(start, CH), :] = product[
                        row * CH : (row + 1) * CH, side * LANES : (side + 1) * LANES
                    ]
        return 0

    lax.fori_loop(0, freqs // FREQ_UNROLL, body, 0)


def slot_numbers(width):
    shape = (CLASSES // 16, 16, width)
    ids = lax.broadcasted_iota(jnp.int32, shape, 0) * 16 + lax.broadcasted_iota(jnp.int32, shape, 1)
    return ids.astype(F32).astype(BF16)


def slots_of(marks):
    classes = lax.shift_right_logical(marks, 2)
    return ((classes & 1) * (CLASSES // 2) + lax.shift_right_logical(classes, 1)).astype(F32)


def piece_of(cross, i, nrows, width):
    sides = [cross[side, pl.ds(i, nrows, stride=CH + PAD), :] for side in range(width // LANES)]
    return jnp.concatenate(sides, axis=1).astype(BF16)


def row_of(ref, i, width):
    return jnp.broadcast_to(ref[pl.ds(i, 1), :][:, :width], (16, width)).astype(BF16)


def add_bins(cross, read_labels, width, weight, slots, nrows, add_sums, counts):
    slot_ids = slot_numbers(width)
    unroll = ROW_UNROLL * CH // width
    one = jnp.ones((), BF16)
    zero = jnp.zeros((), BF16)
    segments = read_labels() & (SEGMENTS - 1)
    first, last = jnp.min(segments), jnp.max(segments)

    def add_segment(segment, _):
        marks = read_labels()
        slots[:, :width] = jnp.where((marks & (SEGMENTS - 1)) == segment, slots_of(marks), -1.0)

        def add_rows(block, _):
            pieces, onehots = [], []
            tally = None
            for part in range(unroll):
                i = block * unroll + part
                pieces.append(piece_of(cross, i, nrows, width))
                row = row_of(slots, i, width)
                onehot = jnp.where(row[None] == slot_ids, one, zero).reshape(CLASSES, width)
                onehots.append(onehot)
                tally = onehot if tally is None else tally + onehot
            add_sums(
                segment,
                lax.dot_general(
                    jnp.concatenate(pieces, axis=1),
                    jnp.concatenate(onehots, axis=1),
                    (((1,), (1,)), ((), ())),
                    preferred_element_type=F32,
                ),
            )
            counts[segment, :, :width] += tally.astype(F32) * weight
            return 0

        lax.fori_loop(0, CH // unroll, add_rows, 0)
        return 0

    lax.fori_loop(first, last + 1, add_segment, 0)


def add_all_bins(cross, slots, segments, width, nrows, add_sums, add_tally, begin=0, end=CH):
    slot_ids = slot_numbers(width)
    unroll = SELF_UNROLL * CH // width
    row_ids = lax.broadcasted_iota(jnp.int32, (16, width), 0).astype(F32).astype(BF16)
    one = jnp.ones((), BF16)
    zero = jnp.zeros((), BF16)

    def add_rows(block, _):
        pieces, onehots = [], []
        for part in range(unroll):
            i = block * unroll + part
            values = piece_of(cross, i, nrows, width).reshape(nrows // 16, 16, width)
            place = row_of(segments, i, width)
            masked = [
                jnp.where(place[None] == jnp.full((), segment, BF16), values, zero).reshape(nrows, width)
                for segment in range(SEGMENTS)
            ]
            masked.append(jnp.where(place == row_ids, one, zero))
            pieces.append(jnp.concatenate(masked, axis=0))
            row = row_of(slots, i, width)
            onehots.append(jnp.where(row[None] == slot_ids, one, zero).reshape(CLASSES, width))
        binned = lax.dot_general(
            jnp.concatenate(pieces, axis=1),
            jnp.concatenate(onehots, axis=1),
            (((1,), (1,)), ((), ())),
            preferred_element_type=F32,
        )
        for segment in range(SEGMENTS):
            add_sums(segment, binned[segment * nrows : (segment + 1) * nrows])
        add_tally(binned[SEGMENTS * nrows :])
        return 0

    lax.fori_loop(begin // unroll, end // unroll, add_rows, 0)


def as_integers(values):
    return values.astype(F32).astype(jnp.int32)


def turned_back(values, side):
    half = values.shape[0] // 2
    sign = (1 - 2 * side).astype(F32)
    return jnp.concatenate([values[:half], values[half:] * sign], axis=0)


def exchange_kernel(
    spectra, pair_bins, after, before, beside, white_out, early_out, labels_before, labels_beside, sums, tally,
    raw, early_raw, labels, sent_labels, white, early, rows, cross, slots, segments,
    local_sem, send_sem, recv_sem,
):
    half = white.shape[1]
    chan, off = lax.axis_index("chan"), lax.axis_index("off")
    count = lax.axis_size("chan")
    low = lax.rem(chan, 2)
    even, odd = (1 - low).astype(F32), low.astype(F32)
    down, up = lax.rem(chan + count - 2, count), lax.rem(chan + 2, count)
    partner = chan + 1 - 2 * low
    load_raw = pltpu.make_async_copy(spectra, raw, local_sem.at[0])
    load_labels = pltpu.make_async_copy(pair_bins.at[0], labels, local_sem.at[1])
    load_labels.start()
    load_raw.start()
    barrier = pltpu.get_barrier_semaphore()
    for neighbour in (partner, down, up):
        pl.semaphore_signal(barrier, inc=1, device_id=(neighbour, off), device_id_type=MESH)
    pl.semaphore_wait(barrier, 3)

    def remote(index, source, target, chan_to):
        return pltpu.make_async_remote_copy(
            src_ref=source,
            dst_ref=target,
            send_sem=send_sem.at[index],
            recv_sem=recv_sem.at[index],
            device_id=(chan_to, off),
            device_id_type=MESH,
        )

    other_half = pl.ds(pl.multiple_of((1 - low) * half, half), half)
    copies = []
    for piece in range(2):
        part = slice(piece * EARLY, (piece + 1) * EARLY)
        copies.append(
            [
                remote(3 * piece, spectra.at[part, other_half, :], beside.at[part], partner),
                remote(3 * piece + 1, spectra.at[part, 0:half, :], after.at[part], down),
                remote(3 * piece + 2, spectra.at[part, half : 2 * half, :], before.at[part], up),
            ]
        )
    for copy in copies[0]:
        copy.start()
    load_labels.wait()
    near, far = labels[1].astype(F32), labels[2].astype(F32)
    near_turned = near.T
    sent_labels[0] = near_turned.astype(BF16)
    sent_labels[1] = far.T.astype(BF16)
    sent_labels[2] = jnp.where(low == 0, near_turned, near).astype(BF16)
    label_copies = [
        remote(6, sent_labels.at[1], labels_before.at[1], up),
        remote(7, sent_labels.at[2], labels_beside, partner),
    ]
    for copy in label_copies:
        copy.start()
    near_copy = remote(8, sent_labels.at[0], labels_before.at[0], up)

    @pl.when(low == 1)
    def _():
        near_copy.start()

    marks = labels[0]
    slots[...] = slots_of(marks)
    segments[...] = (marks & (SEGMENTS - 1)).astype(F32)
    sums[...] = jnp.zeros_like(sums)
    tally[...] = jnp.zeros_like(tally)
    load_raw.wait()
    whiten(raw, rows, white.reshape(2 * half, 2, CH, LANES), True)
    keep = pltpu.make_async_copy(white, white_out, local_sem.at[2])
    keep.start()

    def own(side):
        return lambda freq: white[side, freq].reshape(2 * CH, LANES)

    for side in range(2):
        cross_pairs(own(side), lambda freq, side=side: white[side, freq, 0], cross, half, side * 2 * half)

    def add_self(segment, values):
        sums[segment] += values.reshape(2, 2 * half, CLASSES)

    def add_tally(weight):
        def add(values):
            tally[...] += values * weight

        return add

    bin_self = functools.partial(
        add_all_bins, cross, slots, segments, CH, 4 * half, add_self, add_tally(1.0)
    )
    bin_self(begin=0, end=CH // 2)
    for copy in copies[1]:
        copy.start()
    bin_self(begin=CH // 2, end=CH)

    loads = []
    for index, (copy, block) in enumerate(zip(copies[0], (beside, after, before))):
        copy.wait_recv()
        load = pltpu.make_async_copy(block.at[0:EARLY], early_raw.at[index], local_sem.at[3 + index])
        load.start()
        loads.append(load)
    for index, load in enumerate(loads):
        load.wait()
        whiten(early_raw.at[index], rows, early.at[index], index == 0)
    keep_early = pltpu.make_async_copy(early, early_out, local_sem.at[6])
    keep_early.start()
    for copy in label_copies:
        copy.wait_recv()
    before_far, beside_near = as_integers(labels_before[1]), as_integers(labels_beside[...])
    own_near, own_far = labels[1], labels[2]
    marks = jnp.concatenate(
        [
            jnp.where(low == 0, own_near, beside_near)[:, :LANES],
            jnp.where(low == 0, own_far, before_far)[:, :LANES],
        ],
        axis=1,
    )
    slots[...] = slots_of(marks)
    segments[...] = (marks & (SEGMENTS - 1)).astype(F32)

    def add_to(side):
        def add(segment, values):
            sums[segment, side] += turned_back(values, side)

        return add

    cross_pairs(
        own(low),
        lambda freq: jnp.concatenate([early[0, freq, 0], early[1 + low, freq, 0]], axis=0),
        cross,
        half,
    )
    add_all_bins(cross, slots, segments, CH, 2 * half, add_to(low), add_tally(even))
    marks = jnp.where(low == 0, before_far, own_far)[:, :LANES]
    slots[:, :LANES] = slots_of(marks)
    segments[:, :LANES] = (marks & (SEGMENTS - 1)).astype(F32)
    cross_pairs(own(1 - low), lambda freq: early[2 - low, freq, 0], cross, half)
    add_all_bins(cross, slots, segments, LANES, 2 * half, add_to(1 - low), add_tally(odd))

    keep.wait()
    keep_early.wait()
    for copy in copies[1]:
        copy.wait_recv()
    for copy in copies[0] + copies[1] + label_copies:
        copy.wait_send()

    @pl.when(low == 1)
    def _():
        near_copy.wait()


def pairs_kernel(
    own, early, beside, after, before, labels, labels_beside, labels_before, sums_in,
    sums, counts, white, blocks, raw, rows, cross, slots, load_sem,
):
    half = own.shape[1]
    loads = [
        pltpu.make_async_copy(block.at[EARLY : 2 * EARLY], raw.at[index], load_sem.at[index])
        for index, block in enumerate((beside, after, before))
    ]
    load_own = pltpu.make_async_copy(own, white, load_sem.at[3])
    load_early = pltpu.make_async_copy(early, blocks.at[0], load_sem.at[4])
    for load in loads + [load_own, load_early]:
        load.start()
    sums[...] = sums_in[...]
    counts[...] = jnp.zeros_like(counts)
    for index, load in enumerate(loads):
        load.wait()
        whiten(raw.at[index], rows, blocks.at[1, index], index == 0)
    load_own.wait()
    low = lax.rem(lax.axis_index("chan"), 2)
    counted = (lax.axis_index("off") == 0).astype(F32)
    even = (1 - low).astype(F32) * counted
    odd = low.astype(F32) * counted

    def own_rows(side):
        return lambda freq: white[side, freq].reshape(2 * CH, LANES)

    def late_pair(freq):
        return jnp.concatenate([blocks[1, 0, freq, 0], blocks[1, 1 + low, freq, 0]], axis=0)

    def both_halves(index, row):
        return lambda freq: jnp.concatenate([blocks[0, index, freq, row], blocks[1, index, freq, row]], axis=0)

    def beside_rows(freq):
        return jnp.concatenate([both_halves(0, 0)(freq), both_halves(0, 1)(freq)], axis=0)

    def late_labels():
        near = jnp.where(low == 0, labels[1, :, LANES:], as_integers(labels_beside[:, LANES:]))
        far = jnp.where(low == 0, labels[2, :, LANES:], as_integers(labels_before[1, :, LANES:]))
        return jnp.concatenate([near, far], axis=1)

    def moved_labels():
        return as_integers(jnp.where(low == 0, labels_beside[...].astype(F32), labels_before[0].astype(F32)))

    def other_labels():
        return jnp.where(low == 0, as_integers(labels_before[1, :, LANES:]), labels[2, :, LANES:])

    def add_to(side):
        def add(segment, values):
            sums[segment, side] += turned_back(values, side)

        return add

    cross_pairs(own_rows(low), late_pair, cross, half)
    add_bins(cross, late_labels, CH, even, slots, 2 * half, add_to(low), counts)
    cross_pairs(own_rows(1 - low), lambda freq: blocks[1, 2 - low, freq, 0], cross, half)
    add_bins(cross, other_labels, LANES, odd, slots, 2 * half, add_to(1 - low), counts)
    load_early.wait()
    cross_pairs(beside_rows, both_halves(1 + low, 0), cross, half)
    add_bins(cross, moved_labels, CH, even, slots, 2 * half, add_to(low), counts)


def reduce_kernel(
    sums, counts, self_tally, table, out, parts, near_in, far_out, far_in, near_send, near_recv, far_send, far_recv
):
    chan, off = lax.axis_index("chan"), lax.axis_index("off")
    low, high = lax.rem(chan, 2), lax.div(chan, 2)
    near = off * 2 + low

    def near_device(step):
        index = lax.rem(near + step, NEAR)
        return index, (high * 2 + lax.rem(index, 2), lax.div(index, 2))

    def far_device(step):
        index = lax.rem(high + step, FAR)
        return index, (index * 2 + low, off)

    barrier = pltpu.get_barrier_semaphore()

    def greet_near(step, _):
        pl.semaphore_signal(barrier, inc=1, device_id=near_device(step)[1], device_id_type=MESH)
        return 0

    def greet_far(step, _):
        pl.semaphore_signal(barrier, inc=1, device_id=far_device(step)[1], device_id_type=MESH)
        return 0

    lax.fori_loop(1, NEAR, greet_near, 0)
    lax.fori_loop(1, FAR, greet_far, 0)
    ones = jnp.ones((COUNT_ROWS, CH), F32)
    for segment in range(SEGMENTS):
        trace = lax.dot_general(
            sums[segment].reshape(table.shape[1], CLASSES),
            table[off],
            (((0,), (0,)), ((), ())),
            precision=lax.Precision.HIGHEST,
            preferred_element_type=F32,
        )
        tally = lax.dot_general(
            ones,
            counts[segment],
            (((1,), (1,)), ((), ())),
            precision=lax.Precision.HIGHEST,
            preferred_element_type=F32,
        )
        own = self_tally[segment : segment + 1, :] * (off == 0).astype(F32)
        tally = tally + jnp.broadcast_to(own, tally.shape)
        tally = jnp.concatenate([tally, jnp.zeros((COUNT_ROWS, LANES - CLASSES), F32)], axis=1)
        for part in range(2):
            parts[segment * 2 + part, :FAR, :] = trace[part * FAR : (part + 1) * FAR]
            parts[segment * 2 + part, FAR:, :] = tally
    pl.semaphore_wait(barrier, FAR - 1 + NEAR - 1)

    def near_copy(step):
        index, device = near_device(step)
        return pltpu.make_async_remote_copy(
            src_ref=parts.at[index],
            dst_ref=near_in.at[step - 1],
            send_sem=near_send.at[step - 1],
            recv_sem=near_recv.at[step - 1],
            device_id=device,
            device_id_type=MESH,
        )

    def far_copy(step):
        index, device = far_device(step)
        return pltpu.make_async_remote_copy(
            src_ref=far_out.at[index],
            dst_ref=far_in.at[step - 1],
            send_sem=far_send.at[step - 1],
            recv_sem=far_recv.at[step - 1],
            device_id=device,
            device_id_type=MESH,
        )

    def start_near(step, _):
        near_copy(step).start()
        return 0

    def start_far(step, _):
        far_copy(step).start()
        return 0

    lax.fori_loop(1, NEAR, start_near, 0)

    def add_near(step, total):
        near_copy(step).wait_recv()
        return total + near_in[step - 1]

    total = lax.fori_loop(1, NEAR, add_near, parts[near])
    for row in range(FAR):
        far_out[row] = jnp.concatenate([total[row : row + 1], total[FAR : FAR + 1]], axis=1)
    lax.fori_loop(1, FAR, start_far, 0)

    def add_far(step, total):
        far_copy(step).wait_recv()
        return total + far_in[step - 1]

    total = lax.fori_loop(1, FAR, add_far, far_out[high])
    lane = lax.broadcasted_iota(jnp.int32, (1, LANES), 1)
    count = jnp.sum(jnp.where(lane == low * FAR + high, total[:, LANES:], 0.0), axis=1, keepdims=True)
    out[...] = total[:, :LANES] / jnp.sqrt(jnp.maximum(count, 1.0))

    def end_near(step, _):
        near_copy(step).wait_send()
        return 0

    def end_far(step, _):
        far_copy(step).wait_send()
        return 0

    lax.fori_loop(1, NEAR, end_near, 0)
    lax.fori_loop(1, FAR, end_far, 0)


def lag_tables(groups, freqs, lags):
    nfreq = groups * freqs
    shifts = np.arange(lags) - lags // 2
    theta = math.pi * np.mod(np.arange(nfreq)[:, None] * shifts[None, :], 2 * nfreq) / nfreq
    table = np.stack([np.cos(theta), -np.sin(theta)]).reshape(2, groups, 2, freqs // 2, lags)
    table = table.transpose(1, 2, 0, 3, 4).reshape(groups, 2 * freqs, lags)
    return jnp.asarray((table / HALF).astype(np.float32))


def on_device(spectra, pair_bins):
    freqs = spectra.shape[1]
    half = freqs // 2
    vmem_limit = 56 * 1024 * 1024
    white_shape = jax.ShapeDtypeStruct((2, half, 2, CH, LANES), BF16)
    early_shape = jax.ShapeDtypeStruct((3, half, 2, EARLY, LANES), BF16)
    block_shape = jax.ShapeDtypeStruct((CH, half, LANES), BF16)
    sums_shape = jax.ShapeDtypeStruct((SEGMENTS, 2, 2 * half, CLASSES), F32)
    counts_shape = jax.ShapeDtypeStruct((SEGMENTS, CLASSES, CH), F32)
    square = pltpu.VMEM((CH, CH), F32)

    after, before, beside, white, early, labels_before, labels_beside, sums, tally = pl.pallas_call(
        exchange_kernel,
        out_shape=[
            block_shape,
            block_shape,
            block_shape,
            white_shape,
            early_shape,
            jax.ShapeDtypeStruct((2, CH, CH), BF16),
            jax.ShapeDtypeStruct((CH, CH), BF16),
            sums_shape,
            jax.ShapeDtypeStruct((16, CLASSES), F32),
        ],
        in_specs=[ANY] * 2,
        out_specs=[ANY] * 5 + [VMEM] * 4,
        scratch_shapes=[
            pltpu.VMEM(spectra.shape, BF16),
            pltpu.VMEM((3, EARLY, half, LANES), BF16),
            pltpu.VMEM(pair_bins.shape[1:], jnp.int32),
            pltpu.VMEM((3, CH, CH), BF16),
            pltpu.VMEM(white_shape.shape, BF16),
            pltpu.VMEM(early_shape.shape, BF16),
            pltpu.VMEM((CH * (freqs + PAD), LANES), F32),
            pltpu.VMEM((2, 2 * freqs * (CH + PAD), LANES), F32),
            square,
            square,
            DMA((7,)),
            DMA((9,)),
            DMA((9,)),
        ],
        compiler_params=pltpu.CompilerParams(
            collective_id=1, has_side_effects=True, vmem_limit_bytes=vmem_limit
        ),
    )(spectra, pair_bins)
    sums, counts = pl.pallas_call(
        pairs_kernel,
        out_shape=[sums_shape, counts_shape],
        in_specs=[ANY] * 5 + [VMEM] * 4,
        out_specs=[VMEM] * 2,
        scratch_shapes=[
            pltpu.VMEM(white_shape.shape, BF16),
            pltpu.VMEM((2,) + early_shape.shape, BF16),
            pltpu.VMEM((3, EARLY, half, LANES), BF16),
            pltpu.VMEM((EARLY * (half + PAD), LANES), F32),
            pltpu.VMEM((2, 2 * half * (CH + PAD), LANES), F32),
            square,
            DMA((5,)),
        ],
        compiler_params=pltpu.CompilerParams(vmem_limit_bytes=vmem_limit),
    )(white, early, beside, after, before, pair_bins[0], labels_beside, labels_before, sums)
    return pl.pallas_call(
        reduce_kernel,
        out_shape=jax.ShapeDtypeStruct((1, LANES), F32),
        in_specs=[VMEM] * 4,
        out_specs=VMEM,
        scratch_shapes=[
            pltpu.VMEM((NEAR, FAR + COUNT_ROWS, LANES), F32),
            pltpu.VMEM((NEAR - 1, FAR + COUNT_ROWS, LANES), F32),
            pltpu.VMEM((FAR, 1, 2 * LANES), F32),
            pltpu.VMEM((FAR - 1, 1, 2 * LANES), F32),
            DMA((NEAR - 1,)),
            DMA((NEAR - 1,)),
            DMA((FAR - 1,)),
            DMA((FAR - 1,)),
        ],
        compiler_params=pltpu.CompilerParams(collective_id=0, has_side_effects=True),
    )(sums, counts, tally, lag_tables(lax.axis_size("off"), freqs, LANES))


def solution(mesh):
    in_specs = (P("chan", "off", None), P("chan", None, None, None))
    out_specs = P(("chan", "off"), None)
    return jax.shard_map(
        on_device, mesh=mesh, in_specs=in_specs, out_specs=out_specs, check_vma=False
    )
```

```python
import functools
import math

import jax
import jax.numpy as jnp
import numpy as np
from jax import lax
from jax.experimental import pallas as pl
from jax.experimental.pallas import tpu as pltpu
from jax.sharding import PartitionSpec as P

F32 = jnp.float32
BF16 = jnp.bfloat16
MESH = pl.DeviceIdType.MESH
VMEM = pl.BlockSpec(memory_space=pltpu.VMEM)
ANY = pl.BlockSpec(memory_space=pl.ANY)
DMA = pltpu.SemaphoreType.DMA

CH = 256
LANES = 128
EARLY = CH // 2
HALF = LANES // 2
SEGMENTS = 4
CLASSES = 64
PAD = 8
NEAR = 8
FAR = 32
FREQ_UNROLL = 8
ROW_UNROLL = 64
STATIC_UNROLL = 64
COUNT_ROWS = 8


def whiten(raw, rows, white, with_rotated):
    channels, freqs, _ = raw.shape
    step = freqs + PAD
    chunk = 32

    def normalise(block, _):
        values = raw[pl.ds(block * chunk, chunk)].astype(F32)
        meansq = jnp.mean(values * values, axis=-1, keepdims=True)
        scaled = values * lax.rsqrt(meansq + 1e-05)
        for channel in range(chunk):
            start = pl.multiple_of((block * chunk + channel) * step, 8)
            rows[pl.ds(start, freqs), :] = scaled[channel]
        return 0

    lax.fori_loop(0, channels // chunk, normalise, 0)

    def regroup(block, _):
        for part in range(FREQ_UNROLL):
            freq = block * FREQ_UNROLL + part
            values = rows[pl.ds(freq, channels, stride=step), :]
            white[freq, 0] = values.astype(BF16)
            if with_rotated:
                lane = lax.broadcasted_iota(jnp.int32, (channels, LANES), 1)
                turned = pltpu.roll(values, HALF, 1)
                white[freq, 1] = jnp.where(lane < HALF, turned, -turned).astype(BF16)
        return 0

    lax.fori_loop(0, freqs // FREQ_UNROLL, regroup, 0)


def cross_pairs(first, second, cross, freqs, top=0):
    step = CH + PAD

    def body(block, _):
        for part in range(FREQ_UNROLL):
            freq = block * FREQ_UNROLL + part
            product = lax.dot_general(
                first(freq), second(freq), (((1,), (1,)), ((), ())), preferred_element_type=F32
            )
            for row in range(2):
                start = pl.multiple_of((top + freq + row * freqs) * step, 8)
                for side in range(product.shape[1] // LANES):
                    cross[side, pl.ds(start, CH), :] = product[
                        row * CH : (row + 1) * CH, side * LANES : (side + 1) * LANES
                    ]
        return 0

    lax.fori_loop(0, freqs // FREQ_UNROLL, body, 0)


def slot_numbers(width, count=CLASSES):
    shape = (count // 16, 16, width)
    ids = lax.broadcasted_iota(jnp.int32, shape, 0) * 16 + lax.broadcasted_iota(jnp.int32, shape, 1)
    return ids.astype(F32).astype(BF16)


def slots_of(marks):
    classes = lax.shift_right_logical(marks, 2)
    return ((classes & 1) * (CLASSES // 2) + lax.shift_right_logical(classes, 1)).astype(F32)


def piece_of(cross, i, nrows, sides):
    pieces = [cross[side, pl.ds(i, nrows, stride=CH + PAD), :] for side in sides]
    return jnp.concatenate(pieces, axis=1).astype(BF16)


def row_of(ref, i, width):
    return jnp.broadcast_to(ref[pl.ds(i, 1), :][:, :width], (16, width)).astype(BF16)


def add_bins(cross, read_labels, sides, weight, slots, nrows, add_sums, counts):
    width = len(sides) * LANES
    slot_ids = slot_numbers(width)
    unroll = ROW_UNROLL * CH // width
    one = jnp.ones((), BF16)
    zero = jnp.zeros((), BF16)
    segments = read_labels() & (SEGMENTS - 1)
    first, last = jnp.min(segments), jnp.max(segments)

    def add_segment(segment, _):
        marks = read_labels()
        slots[:, :width] = jnp.where((marks & (SEGMENTS - 1)) == segment, slots_of(marks), -1.0)

        def add_rows(block, _):
            pieces, onehots = [], []
            tally = None
            for part in range(unroll):
                i = block * unroll + part
                pieces.append(piece_of(cross, i, nrows, sides))
                row = row_of(slots, i, width)
                onehot = jnp.where(row[None] == slot_ids, one, zero).reshape(CLASSES, width)
                onehots.append(onehot)
                tally = onehot if tally is None else tally + onehot
            add_sums(
                segment,
                lax.dot_general(
                    jnp.concatenate(pieces, axis=1),
                    jnp.concatenate(onehots, axis=1),
                    (((1,), (1,)), ((), ())),
                    preferred_element_type=F32,
                ),
            )
            counts[segment, :, :width] += tally.astype(F32) * weight
            return 0

        lax.fori_loop(0, CH // unroll, add_rows, 0)
        return 0

    lax.fori_loop(first, last + 1, add_segment, 0)


def place_marks(marks, masks, slots, segments):
    width = marks.shape[1]
    groups = SEGMENTS // masks
    segment = marks & (SEGMENTS - 1)
    slots[:, :width] = slots_of(marks) + (CLASSES * (segment & (groups - 1))).astype(F32)
    segments[:, :width] = lax.shift_right_logical(segment, groups // 2).astype(F32)


def add_all_bins(cross, slots, segments, masks, sides, nrows, add_sums, add_tally, begin=0, end=CH):
    width = len(sides) * LANES
    groups = SEGMENTS // masks
    nslots = groups * CLASSES
    slot_ids = slot_numbers(width, nslots)
    unroll = STATIC_UNROLL
    row_ids = lax.broadcasted_iota(jnp.int32, (16, width), 0).astype(F32).astype(BF16)
    one = jnp.ones((), BF16)
    zero = jnp.zeros((), BF16)

    def add_rows(block, _):
        pieces, onehots = [], []
        for part in range(unroll):
            i = block * unroll + part
            values = piece_of(cross, i, nrows, sides).reshape(nrows // 16, 16, width)
            place = row_of(segments, i, width)
            masked = [
                jnp.where(place[None] == jnp.full((), mask, BF16), values, zero).reshape(nrows, width)
                for mask in range(masks)
            ]
            masked.append(jnp.where(place == row_ids, one, zero))
            pieces.append(jnp.concatenate(masked, axis=0))
            row = row_of(slots, i, width)
            onehots.append(jnp.where(row[None] == slot_ids, one, zero).reshape(nslots, width))
        binned = lax.dot_general(
            jnp.concatenate(pieces, axis=1),
            jnp.concatenate(onehots, axis=1),
            (((1,), (1,)), ((), ())),
            preferred_element_type=F32,
        )
        for segment in range(SEGMENTS):
            mask, group = segment // groups, segment % groups
            columns = slice(group * CLASSES, (group + 1) * CLASSES)
            tally_row = masks * nrows + mask
            add_sums(segment, binned[mask * nrows : (mask + 1) * nrows, columns])
            add_tally(segment, binned[tally_row : tally_row + 1, columns])
        return 0

    lax.fori_loop(begin // unroll, end // unroll, add_rows, 0)


def as_integers(values):
    return values.astype(F32).astype(jnp.int32)


def turned_back(values, side):
    half = values.shape[0] // 2
    sign = (1 - 2 * side).astype(F32)
    return jnp.concatenate([values[:half], values[half:] * sign], axis=0)


def exchange_kernel(
    spectra, pair_bins, after, before, beside, white_out, early_out, labels_before, labels_beside, sums, tally,
    raw, early_raw, labels, sent_labels, white, early, rows, cross, slots, segments,
    local_sem, send_sem, recv_sem,
):
    half = white.shape[1]
    chan, off = lax.axis_index("chan"), lax.axis_index("off")
    count = lax.axis_size("chan")
    low = lax.rem(chan, 2)
    even, odd = (1 - low).astype(F32), low.astype(F32)
    down, up = lax.rem(chan + count - 2, count), lax.rem(chan + 2, count)
    partner = chan + 1 - 2 * low
    load_raw = pltpu.make_async_copy(spectra, raw, local_sem.at[0])
    load_labels = pltpu.make_async_copy(pair_bins.at[0], labels, local_sem.at[1])
    load_labels.start()
    load_raw.start()
    barrier = pltpu.get_barrier_semaphore()
    for neighbour in (partner, down, up):
        pl.semaphore_signal(barrier, inc=1, device_id=(neighbour, off), device_id_type=MESH)
    pl.semaphore_wait(barrier, 3)

    def remote(index, source, target, chan_to):
        return pltpu.make_async_remote_copy(
            src_ref=source,
            dst_ref=target,
            send_sem=send_sem.at[index],
            recv_sem=recv_sem.at[index],
            device_id=(chan_to, off),
            device_id_type=MESH,
        )

    other_half = pl.ds(pl.multiple_of((1 - low) * half, half), half)
    copies = []
    for piece in range(2):
        part = slice(piece * EARLY, (piece + 1) * EARLY)
        copies.append(
            [
                remote(3 * piece, spectra.at[part, other_half, :], beside.at[part], partner),
                remote(3 * piece + 1, spectra.at[part, 0:half, :], after.at[part], down),
                remote(3 * piece + 2, spectra.at[part, half : 2 * half, :], before.at[part], up),
            ]
        )
    for copy in copies[0]:
        copy.start()
    load_labels.wait()
    near, far = labels[1].astype(F32), labels[2].astype(F32)
    near_turned = near.T
    sent_labels[0] = near_turned.astype(BF16)
    sent_labels[1] = far.T.astype(BF16)
    sent_labels[2] = jnp.where(low == 0, near_turned, near).astype(BF16)
    label_copies = [
        remote(6, sent_labels.at[1], labels_before.at[1], up),
        remote(7, sent_labels.at[2], labels_beside, partner),
    ]
    for copy in label_copies:
        copy.start()
    near_copy = remote(8, sent_labels.at[0], labels_before.at[0], up)

    @pl.when(low == 1)
    def _():
        near_copy.start()

    place_marks(labels[0], 2, slots, segments)
    sums[...] = jnp.zeros_like(sums)
    tally[...] = jnp.zeros_like(tally)
    load_raw.wait()
    whiten(raw, rows, white.reshape(2 * half, 2, CH, LANES), True)
    keep = pltpu.make_async_copy(white, white_out, local_sem.at[2])
    keep.start()

    def own(side):
        return lambda freq: white[side, freq].reshape(2 * CH, LANES)

    for side in range(2):
        cross_pairs(own(side), lambda freq, side=side: white[side, freq, 0], cross, half, side * 2 * half)

    def add_self(segment, values):
        sums[segment] += values.reshape(2, 2 * half, CLASSES)

    def add_tally(weight):
        def add(segment, values):
            tally[segment : segment + 1, :] += values * weight

        return add

    bin_self = functools.partial(
        add_all_bins, cross, slots, segments, 2, (0, 1), 4 * half, add_self, add_tally(1.0)
    )
    bin_self(begin=0, end=CH // 2)
    for copy in copies[1]:
        copy.start()
    bin_self(begin=CH // 2, end=CH)

    loads = []
    for index, (copy, block) in enumerate(zip(copies[0], (beside, after, before))):
        copy.wait_recv()
        load = pltpu.make_async_copy(block.at[0:EARLY], early_raw.at[index], local_sem.at[3 + index])
        load.start()
        loads.append(load)
    for index, load in enumerate(loads):
        load.wait()
        whiten(early_raw.at[index], rows, early.at[index], index == 0)
    keep_early = pltpu.make_async_copy(early, early_out, local_sem.at[6])
    keep_early.start()
    for copy in label_copies:
        copy.wait_recv()
    before_far, beside_near = as_integers(labels_before[1]), as_integers(labels_beside[...])
    own_near, own_far = labels[1], labels[2]
    marks = jnp.concatenate(
        [
            jnp.where(low == 0, own_near, beside_near)[:, :LANES],
            jnp.where(low == 0, own_far, before_far)[:, :LANES],
        ],
        axis=1,
    )
    place_marks(marks, SEGMENTS, slots, segments)

    def add_to(side):
        def add(segment, values):
            sums[segment, side] += turned_back(values, side)

        return add

    cross_pairs(
        own(low),
        lambda freq: jnp.concatenate([early[0, freq, 0], early[1 + low, freq, 0]], axis=0),
        cross,
        half,
    )
    add_all_bins(cross, slots, segments, SEGMENTS, (0, 1), 2 * half, add_to(low), add_tally(even))
    marks = jnp.where(low == 0, before_far, own_far)[:, :LANES]
    place_marks(marks, SEGMENTS, slots, segments)
    cross_pairs(own(1 - low), lambda freq: early[2 - low, freq, 0], cross, half)
    add_all_bins(cross, slots, segments, SEGMENTS, (0,), 2 * half, add_to(1 - low), add_tally(odd))

    keep.wait()
    keep_early.wait()
    for copy in copies[1]:
        copy.wait_recv()
    for copy in copies[0] + copies[1] + label_copies:
        copy.wait_send()

    @pl.when(low == 1)
    def _():
        near_copy.wait()


def pairs_kernel(
    own, early, beside, after, before, labels, labels_beside, labels_before, sums_in,
    sums, counts, white, blocks, raw, rows, cross, slots, load_sem,
):
    half = own.shape[1]
    loads = [
        pltpu.make_async_copy(block.at[EARLY : 2 * EARLY], raw.at[index], load_sem.at[index])
        for index, block in enumerate((beside, after, before))
    ]
    load_own = pltpu.make_async_copy(own, white, load_sem.at[3])
    load_early = pltpu.make_async_copy(early, blocks.at[0], load_sem.at[4])
    for load in loads + [load_own, load_early]:
        load.start()
    sums[...] = sums_in[...]
    counts[...] = jnp.zeros_like(counts)
    for index, load in enumerate(loads):
        load.wait()
        whiten(raw.at[index], rows, blocks.at[1, index], index == 0)
    load_own.wait()
    low = lax.rem(lax.axis_index("chan"), 2)
    counted = (lax.axis_index("off") == 0).astype(F32)
    even = (1 - low).astype(F32) * counted
    odd = low.astype(F32) * counted

    def own_rows(side):
        return lambda freq: white[side, freq].reshape(2 * CH, LANES)

    def late_pair(freq):
        return jnp.concatenate([blocks[1, 0, freq, 0], blocks[1, 1 + low, freq, 0]], axis=0)

    def both_halves(index, row):
        return lambda freq: jnp.concatenate([blocks[0, index, freq, row], blocks[1, index, freq, row]], axis=0)

    def beside_rows(freq):
        return jnp.concatenate([both_halves(0, 0)(freq), both_halves(0, 1)(freq)], axis=0)

    def near_labels():
        return jnp.where(low == 0, labels[1, :, LANES:], as_integers(labels_beside[:, LANES:]))

    def far_labels():
        return jnp.where(low == 0, labels[2, :, LANES:], as_integers(labels_before[1, :, LANES:]))

    def moved_labels():
        return as_integers(jnp.where(low == 0, labels_beside[...].astype(F32), labels_before[0].astype(F32)))

    def other_labels():
        return jnp.where(low == 0, as_integers(labels_before[1, :, LANES:]), labels[2, :, LANES:])

    def add_to(side):
        def add(segment, values):
            sums[segment, side] += turned_back(values, side)

        return add

    cross_pairs(own_rows(low), late_pair, cross, half)
    add_bins(cross, near_labels, (0,), even, slots, 2 * half, add_to(low), counts)
    add_bins(cross, far_labels, (1,), even, slots, 2 * half, add_to(low), counts)
    cross_pairs(own_rows(1 - low), lambda freq: blocks[1, 2 - low, freq, 0], cross, half)
    add_bins(cross, other_labels, (0,), odd, slots, 2 * half, add_to(1 - low), counts)
    load_early.wait()
    cross_pairs(beside_rows, both_halves(1 + low, 0), cross, half)
    add_bins(cross, moved_labels, (0, 1), even, slots, 2 * half, add_to(low), counts)


def reduce_kernel(
    sums, counts, self_tally, table, out, parts, near_in, far_out, far_in, near_send, near_recv, far_send, far_recv
):
    chan, off = lax.axis_index("chan"), lax.axis_index("off")
    low, high = lax.rem(chan, 2), lax.div(chan, 2)
    near = off * 2 + low

    def near_device(step):
        index = lax.rem(near + step, NEAR)
        return index, (high * 2 + lax.rem(index, 2), lax.div(index, 2))

    def far_device(step):
        index = lax.rem(high + step, FAR)
        return index, (index * 2 + low, off)

    barrier = pltpu.get_barrier_semaphore()

    def greet_near(step, _):
        pl.semaphore_signal(barrier, inc=1, device_id=near_device(step)[1], device_id_type=MESH)
        return 0

    def greet_far(step, _):
        pl.semaphore_signal(barrier, inc=1, device_id=far_device(step)[1], device_id_type=MESH)
        return 0

    lax.fori_loop(1, NEAR, greet_near, 0)
    lax.fori_loop(1, FAR, greet_far, 0)
    ones = jnp.ones((COUNT_ROWS, CH), F32)
    for segment in range(SEGMENTS):
        trace = lax.dot_general(
            sums[segment].reshape(table.shape[1], CLASSES),
            table[off],
            (((0,), (0,)), ((), ())),
            precision=lax.Precision.HIGHEST,
            preferred_element_type=F32,
        )
        tally = lax.dot_general(
            ones,
            counts[segment],
            (((1,), (1,)), ((), ())),
            precision=lax.Precision.HIGHEST,
            preferred_element_type=F32,
        )
        own = self_tally[segment : segment + 1, :] * (off == 0).astype(F32)
        tally = tally + jnp.broadcast_to(own, tally.shape)
        tally = jnp.concatenate([tally, jnp.zeros((COUNT_ROWS, LANES - CLASSES), F32)], axis=1)
        for part in range(2):
            parts[segment * 2 + part, :FAR, :] = trace[part * FAR : (part + 1) * FAR]
            parts[segment * 2 + part, FAR:, :] = tally
    pl.semaphore_wait(barrier, FAR - 1 + NEAR - 1)

    def near_copy(step):
        index, device = near_device(step)
        return pltpu.make_async_remote_copy(
            src_ref=parts.at[index],
            dst_ref=near_in.at[step - 1],
            send_sem=near_send.at[step - 1],
            recv_sem=near_recv.at[step - 1],
            device_id=device,
            device_id_type=MESH,
        )

    def far_copy(step):
        index, device = far_device(step)
        return pltpu.make_async_remote_copy(
            src_ref=far_out.at[index],
            dst_ref=far_in.at[step - 1],
            send_sem=far_send.at[step - 1],
            recv_sem=far_recv.at[step - 1],
            device_id=device,
            device_id_type=MESH,
        )

    def start_near(step, _):
        near_copy(step).start()
        return 0

    def start_far(step, _):
        far_copy(step).start()
        return 0

    lax.fori_loop(1, NEAR, start_near, 0)

    def add_near(step, total):
        near_copy(step).wait_recv()
        return total + near_in[step - 1]

    total = lax.fori_loop(1, NEAR, add_near, parts[near])
    for row in range(FAR):
        far_out[row] = jnp.concatenate([total[row : row + 1], total[FAR : FAR + 1]], axis=1)
    lax.fori_loop(1, FAR, start_far, 0)

    def add_far(step, total):
        far_copy(step).wait_recv()
        return total + far_in[step - 1]

    total = lax.fori_loop(1, FAR, add_far, far_out[high])
    lane = lax.broadcasted_iota(jnp.int32, (1, LANES), 1)
    count = jnp.sum(jnp.where(lane == low * FAR + high, total[:, LANES:], 0.0), axis=1, keepdims=True)
    out[...] = total[:, :LANES] / jnp.sqrt(jnp.maximum(count, 1.0))

    def end_near(step, _):
        near_copy(step).wait_send()
        return 0

    def end_far(step, _):
        far_copy(step).wait_send()
        return 0

    lax.fori_loop(1, NEAR, end_near, 0)
    lax.fori_loop(1, FAR, end_far, 0)


def lag_tables(groups, freqs, lags):
    nfreq = groups * freqs
    shifts = np.arange(lags) - lags // 2
    theta = math.pi * np.mod(np.arange(nfreq)[:, None] * shifts[None, :], 2 * nfreq) / nfreq
    table = np.stack([np.cos(theta), -np.sin(theta)]).reshape(2, groups, 2, freqs // 2, lags)
    table = table.transpose(1, 2, 0, 3, 4).reshape(groups, 2 * freqs, lags)
    return jnp.asarray((table / HALF).astype(np.float32))


def on_device(spectra, pair_bins):
    freqs = spectra.shape[1]
    half = freqs // 2
    vmem_limit = 56 * 1024 * 1024
    white_shape = jax.ShapeDtypeStruct((2, half, 2, CH, LANES), BF16)
    early_shape = jax.ShapeDtypeStruct((3, half, 2, EARLY, LANES), BF16)
    block_shape = jax.ShapeDtypeStruct((CH, half, LANES), BF16)
    sums_shape = jax.ShapeDtypeStruct((SEGMENTS, 2, 2 * half, CLASSES), F32)
    counts_shape = jax.ShapeDtypeStruct((SEGMENTS, CLASSES, CH), F32)
    square = pltpu.VMEM((CH, CH), F32)

    after, before, beside, white, early, labels_before, labels_beside, sums, tally = pl.pallas_call(
        exchange_kernel,
        out_shape=[
            block_shape,
            block_shape,
            block_shape,
            white_shape,
            early_shape,
            jax.ShapeDtypeStruct((2, CH, CH), BF16),
            jax.ShapeDtypeStruct((CH, CH), BF16),
            sums_shape,
            jax.ShapeDtypeStruct((16, CLASSES), F32),
        ],
        in_specs=[ANY] * 2,
        out_specs=[ANY] * 5 + [VMEM] * 4,
        scratch_shapes=[
            pltpu.VMEM(spectra.shape, BF16),
            pltpu.VMEM((3, EARLY, half, LANES), BF16),
            pltpu.VMEM(pair_bins.shape[1:], jnp.int32),
            pltpu.VMEM((3, CH, CH), BF16),
            pltpu.VMEM(white_shape.shape, BF16),
            pltpu.VMEM(early_shape.shape, BF16),
            pltpu.VMEM((CH * (freqs + PAD), LANES), F32),
            pltpu.VMEM((2, 2 * freqs * (CH + PAD), LANES), F32),
            square,
            square,
            DMA((7,)),
            DMA((9,)),
            DMA((9,)),
        ],
        compiler_params=pltpu.CompilerParams(
            collective_id=1, has_side_effects=True, vmem_limit_bytes=vmem_limit
        ),
    )(spectra, pair_bins)
    sums, counts = pl.pallas_call(
        pairs_kernel,
        out_shape=[sums_shape, counts_shape],
        in_specs=[ANY] * 5 + [VMEM] * 4,
        out_specs=[VMEM] * 2,
        scratch_shapes=[
            pltpu.VMEM(white_shape.shape, BF16),
            pltpu.VMEM((2,) + early_shape.shape, BF16),
            pltpu.VMEM((3, EARLY, half, LANES), BF16),
            pltpu.VMEM((EARLY * (half + PAD), LANES), F32),
            pltpu.VMEM((2, 2 * half * (CH + PAD), LANES), F32),
            square,
            DMA((5,)),
        ],
        compiler_params=pltpu.CompilerParams(vmem_limit_bytes=vmem_limit),
    )(white, early, beside, after, before, pair_bins[0], labels_beside, labels_before, sums)
    return pl.pallas_call(
        reduce_kernel,
        out_shape=jax.ShapeDtypeStruct((1, LANES), F32),
        in_specs=[VMEM] * 4,
        out_specs=VMEM,
        scratch_shapes=[
            pltpu.VMEM((NEAR, FAR + COUNT_ROWS, LANES), F32),
            pltpu.VMEM((NEAR - 1, FAR + COUNT_ROWS, LANES), F32),
            pltpu.VMEM((FAR, 1, 2 * LANES), F32),
            pltpu.VMEM((FAR - 1, 1, 2 * LANES), F32),
            DMA((NEAR - 1,)),
            DMA((NEAR - 1,)),
            DMA((FAR - 1,)),
            DMA((FAR - 1,)),
        ],
        compiler_params=pltpu.CompilerParams(collective_id=0, has_side_effects=True),
    )(sums, counts, tally, lag_tables(lax.axis_size("off"), freqs, LANES))


def solution(mesh):
    in_specs = (P("chan", "off", None), P("chan", None, None, None))
    out_specs = P(("chan", "off"), None)
    return jax.shard_map(
        on_device, mesh=mesh, in_specs=in_specs, out_specs=out_specs, check_vma=False
    )
```

```python
import functools
import math

import jax
import jax.numpy as jnp
import numpy as np
from jax import lax
from jax.experimental import pallas as pl
from jax.experimental.pallas import tpu as pltpu
from jax.sharding import PartitionSpec as P

F32 = jnp.float32
BF16 = jnp.bfloat16
MESH = pl.DeviceIdType.MESH
VMEM = pl.BlockSpec(memory_space=pltpu.VMEM)
ANY = pl.BlockSpec(memory_space=pl.ANY)
DMA = pltpu.SemaphoreType.DMA

CH = 256
LANES = 128
EARLY = CH // 2
HALF = LANES // 2
SEGMENTS = 4
CLASSES = 64
PAD = 8
NEAR = 8
FAR = 32
FREQ_UNROLL = 8
STATIC_UNROLL = 64
COUNT_ROWS = 8


def whiten(raw, rows, white, with_rotated):
    channels, freqs, _ = raw.shape
    step = freqs + PAD
    chunk = 32

    def normalise(block, _):
        values = raw[pl.ds(block * chunk, chunk)].astype(F32)
        meansq = jnp.mean(values * values, axis=-1, keepdims=True)
        scaled = values * lax.rsqrt(meansq + 1e-05)
        for channel in range(chunk):
            start = pl.multiple_of((block * chunk + channel) * step, 8)
            rows[pl.ds(start, freqs), :] = scaled[channel]
        return 0

    lax.fori_loop(0, channels // chunk, normalise, 0)

    def regroup(block, _):
        for part in range(FREQ_UNROLL):
            freq = block * FREQ_UNROLL + part
            values = rows[pl.ds(freq, channels, stride=step), :]
            white[freq, 0] = values.astype(BF16)
            if with_rotated:
                lane = lax.broadcasted_iota(jnp.int32, (channels, LANES), 1)
                turned = pltpu.roll(values, HALF, 1)
                white[freq, 1] = jnp.where(lane < HALF, turned, -turned).astype(BF16)
        return 0

    lax.fori_loop(0, freqs // FREQ_UNROLL, regroup, 0)


def cross_pairs(first, second, cross, freqs, top=0):
    step = CH + PAD

    def body(block, _):
        for part in range(FREQ_UNROLL):
            freq = block * FREQ_UNROLL + part
            product = lax.dot_general(
                first(freq), second(freq), (((1,), (1,)), ((), ())), preferred_element_type=F32
            )
            for row in range(2):
                start = pl.multiple_of((top + freq + row * freqs) * step, 8)
                for side in range(product.shape[1] // LANES):
                    cross[side, pl.ds(start, CH), :] = product[
                        row * CH : (row + 1) * CH, side * LANES : (side + 1) * LANES
                    ]
        return 0

    lax.fori_loop(0, freqs // FREQ_UNROLL, body, 0)


def slot_numbers(width, count=CLASSES):
    shape = (count // 16, 16, width)
    ids = lax.broadcasted_iota(jnp.int32, shape, 0) * 16 + lax.broadcasted_iota(jnp.int32, shape, 1)
    return ids.astype(F32).astype(BF16)


def slots_of(marks):
    classes = lax.shift_right_logical(marks, 2)
    return ((classes & 1) * (CLASSES // 2) + lax.shift_right_logical(classes, 1)).astype(F32)


def piece_of(cross, i, nrows, sides):
    pieces = [cross[side, pl.ds(i, nrows, stride=CH + PAD), :] for side in sides]
    return jnp.concatenate(pieces, axis=1).astype(BF16)


def row_of(ref, i, width):
    return jnp.broadcast_to(ref[pl.ds(i, 1), :][:, :width], (16, width)).astype(BF16)


def place_marks(marks, masks, slots, segments):
    width = marks.shape[1]
    groups = SEGMENTS // masks
    segment = marks & (SEGMENTS - 1)
    slots[:, :width] = slots_of(marks) + (CLASSES * (segment & (groups - 1))).astype(F32)
    segments[:, :width] = lax.shift_right_logical(segment, groups // 2).astype(F32)


def add_all_bins(cross, slots, segments, masks, sides, nrows, add_sums, add_tally, begin=0, end=CH):
    width = len(sides) * LANES
    groups = SEGMENTS // masks
    nslots = groups * CLASSES
    slot_ids = slot_numbers(width, nslots)
    unroll = STATIC_UNROLL
    row_ids = lax.broadcasted_iota(jnp.int32, (16, width), 0).astype(F32).astype(BF16)
    one = jnp.ones((), BF16)
    zero = jnp.zeros((), BF16)

    def add_rows(block, _):
        pieces, onehots = [], []
        for part in range(unroll):
            i = block * unroll + part
            values = piece_of(cross, i, nrows, sides).reshape(nrows // 16, 16, width)
            place = row_of(segments, i, width)
            masked = [
                jnp.where(place[None] == jnp.full((), mask, BF16), values, zero).reshape(nrows, width)
                for mask in range(masks)
            ]
            masked.append(jnp.where(place == row_ids, one, zero))
            pieces.append(jnp.concatenate(masked, axis=0))
            row = row_of(slots, i, width)
            onehots.append(jnp.where(row[None] == slot_ids, one, zero).reshape(nslots, width))
        binned = lax.dot_general(
            jnp.concatenate(pieces, axis=1),
            jnp.concatenate(onehots, axis=1),
            (((1,), (1,)), ((), ())),
            preferred_element_type=F32,
        )
        for segment in range(SEGMENTS):
            mask, group = segment // groups, segment % groups
            columns = slice(group * CLASSES, (group + 1) * CLASSES)
            tally_row = masks * nrows + mask
            add_sums(segment, binned[mask * nrows : (mask + 1) * nrows, columns])
            add_tally(segment, binned[tally_row : tally_row + 1, columns])
        return 0

    lax.fori_loop(begin // unroll, end // unroll, add_rows, 0)


def as_integers(values):
    return values.astype(F32).astype(jnp.int32)


def network_kernel(
    spectra, pair_bins, table, out,
    raw, across_raw, beside_raw, labels, sent_labels, across_labels, beside_labels, white, across, beside,
    rows, cross, slots, segments, sums, tally, parts, near_in, far_out, far_in,
    local_sem, send_sem, recv_sem, near_send, near_recv, far_send, far_recv,
):
    freqs = raw.shape[1]
    chan, off = lax.axis_index("chan"), lax.axis_index("off")
    count = lax.axis_size("chan")
    low, high = lax.rem(chan, 2), lax.div(chan, 2)
    core = lax.rem(off, 2)
    heavy = low == core
    light = low != core
    near = off * 2 + low
    target = lax.rem(chan + count - 2 + 4 * core, count)
    partner = chan + 1 - 2 * low

    def near_device(step):
        index = lax.rem(near + step, NEAR)
        return index, (high * 2 + lax.rem(index, 2), lax.div(index, 2))

    def far_device(step):
        index = lax.rem(high + step, FAR)
        return index, (index * 2 + low, off)

    load_labels = pltpu.make_async_copy(pair_bins.at[0], labels, local_sem.at[0])
    load_raw = pltpu.make_async_copy(spectra, raw, local_sem.at[1])
    load_labels.start()
    load_raw.start()
    barrier = pltpu.get_barrier_semaphore()

    def greet_near(step, _):
        pl.semaphore_signal(barrier, inc=1, device_id=near_device(step)[1], device_id_type=MESH)
        return 0

    def greet_far(step, _):
        pl.semaphore_signal(barrier, inc=1, device_id=far_device(step)[1], device_id_type=MESH)
        return 0

    lax.fori_loop(1, FAR, greet_far, 0)
    lax.fori_loop(1, NEAR, greet_near, 0)
    load_labels.wait()
    one_ahead, two_ahead = labels[1].astype(F32), labels[2].astype(F32)
    one_turned = one_ahead.T
    sent_labels[0] = one_turned.astype(BF16)
    sent_labels[1] = two_ahead.T.astype(BF16)
    sent_labels[2] = jnp.where(core == 0, one_ahead, one_turned).astype(BF16)

    @pl.when(core == 0)
    def _():
        across_labels[0] = one_ahead.astype(BF16)
        across_labels[1] = two_ahead.astype(BF16)

    pl.semaphore_wait(barrier, FAR - 1 + NEAR - 1)

    def remote(index, source, landing, chan_to):
        return pltpu.make_async_remote_copy(
            src_ref=source,
            dst_ref=landing,
            send_sem=send_sem.at[index],
            recv_sem=recv_sem.at[index],
            device_id=(chan_to, off),
            device_id_type=MESH,
        )

    pieces = [slice(piece * EARLY, (piece + 1) * EARLY) for piece in range(2)]
    across_copies = [remote(i, spectra.at[part], across_raw.at[part], target) for i, part in enumerate(pieces)]
    beside_copies = [remote(2 + i, spectra.at[part], beside_raw.at[part], partner) for i, part in enumerate(pieces)]
    beside_copies.append(remote(4, sent_labels.at[2], beside_labels, partner))
    two_copy = remote(5, sent_labels.at[1], across_labels.at[1], target)
    one_copy = remote(6, sent_labels.at[0], across_labels.at[0], target)
    across_copies[0].start()

    @pl.when(light)
    def _():
        beside_copies[0].start()
        beside_copies[2].start()

    @pl.when(core == 1)
    def _():
        two_copy.start()

    @pl.when(jnp.logical_and(core == 1, low == 1))
    def _():
        one_copy.start()

    place_marks(labels[0], 2, slots, segments)
    sums[...] = jnp.zeros_like(sums)
    tally[...] = jnp.zeros_like(tally)
    load_raw.wait()
    whiten(raw, rows, white, True)

    def own(freq):
        return white[freq].reshape(2 * CH, LANES)

    def add_tally(segment, values):
        tally[segment : segment + 1, :] += values

    def add_self(segment, values):
        sums[segment] += values

    sign = (1 - 2 * core).astype(F32)

    def add_pairs(segment, values):
        sums[segment, :freqs] += values[:freqs]
        sums[segment, freqs:] += values[freqs:] * sign

    def bin_pairs(marks):
        place_marks(marks, 2, slots, segments)
        add_all_bins(cross, slots, segments, 2, (0, 1), 2 * freqs, add_pairs, add_tally)

    cross_pairs(own, lambda freq: white[freq, 0], cross, freqs)
    bin_self = functools.partial(
        add_all_bins, cross, slots, segments, 2, (0, 1), 2 * freqs, add_self, add_tally
    )
    bin_self(begin=0, end=CH // 2)
    across_copies[1].start()

    @pl.when(light)
    def _():
        beside_copies[1].start()

    bin_self(begin=CH // 2, end=CH)
    across_copies[0].wait_recv()
    whiten(across_raw.at[pieces[0]], rows, across.at[0], False)

    @pl.when(core == 1)
    def _():
        two_copy.wait_recv()

    def beside_marks():
        return jnp.where(core == 0, labels[1], as_integers(beside_labels[...]))

    def half_marks(piece):
        lanes = slice(piece * LANES, (piece + 1) * LANES)
        return jnp.concatenate([beside_marks()[:, lanes], as_integers(across_labels[1])[:, lanes]], axis=1)

    def half_blocks(piece):
        return lambda freq: jnp.concatenate([beside[piece, freq, 0], across[piece, freq, 0]], axis=0)

    def whole(block, row):
        return lambda freq: jnp.concatenate([block[0, freq, row], block[1, freq, row]], axis=0)

    def beside_rows(freq):
        return jnp.concatenate([whole(beside, 0)(freq), whole(beside, 1)(freq)], axis=0)

    @pl.when(heavy)
    def _():
        beside_copies[0].wait_recv()
        beside_copies[2].wait_recv()
        whiten(beside_raw.at[pieces[0]], rows, beside.at[0], True)
        cross_pairs(own, half_blocks(0), cross, freqs)
        bin_pairs(half_marks(0))

    across_copies[1].wait_recv()
    whiten(across_raw.at[pieces[1]], rows, across.at[1], False)

    @pl.when(heavy)
    def _():
        beside_copies[1].wait_recv()
        whiten(beside_raw.at[pieces[1]], rows, beside.at[1], True)
        cross_pairs(own, half_blocks(1), cross, freqs)
        bin_pairs(half_marks(1))

        @pl.when(core == 1)
        def _():
            one_copy.wait_recv()

        cross_pairs(beside_rows, whole(across, 0), cross, freqs)
        bin_pairs(as_integers(jnp.where(core == 0, beside_labels[...].astype(F32), across_labels[0].astype(F32))))

    @pl.when(light)
    def _():
        cross_pairs(own, whole(across, 0), cross, freqs)
        bin_pairs(as_integers(across_labels[1]))

    counted = (off == 0).astype(F32)
    for segment in range(SEGMENTS):
        trace = lax.dot_general(
            sums[segment],
            table[off],
            (((0,), (0,)), ((), ())),
            precision=lax.Precision.HIGHEST,
            preferred_element_type=F32,
        )
        counts = jnp.broadcast_to(tally[segment : segment + 1, :] * counted, (COUNT_ROWS, CLASSES))
        counts = jnp.concatenate([counts, jnp.zeros((COUNT_ROWS, LANES - CLASSES), F32)], axis=1)
        for part in range(2):
            parts[segment * 2 + part, :FAR, :] = trace[part * FAR : (part + 1) * FAR]
            parts[segment * 2 + part, FAR:, :] = counts

    def near_copy(step):
        index, device = near_device(step)
        return pltpu.make_async_remote_copy(
            src_ref=parts.at[index],
            dst_ref=near_in.at[step - 1],
            send_sem=near_send.at[step - 1],
            recv_sem=near_recv.at[step - 1],
            device_id=device,
            device_id_type=MESH,
        )

    def far_copy(step):
        index, device = far_device(step)
        return pltpu.make_async_remote_copy(
            src_ref=far_out.at[index],
            dst_ref=far_in.at[step - 1],
            send_sem=far_send.at[step - 1],
            recv_sem=far_recv.at[step - 1],
            device_id=device,
            device_id_type=MESH,
        )

    def start_near(step, _):
        near_copy(step).start()
        return 0

    def start_far(step, _):
        far_copy(step).start()
        return 0

    lax.fori_loop(1, NEAR, start_near, 0)

    def add_near(step, total):
        near_copy(step).wait_recv()
        return total + near_in[step - 1]

    total = lax.fori_loop(1, NEAR, add_near, parts[near])
    for row in range(FAR):
        far_out[row] = jnp.concatenate([total[row : row + 1], total[FAR : FAR + 1]], axis=1)
    lax.fori_loop(1, FAR, start_far, 0)

    def add_far(step, total):
        far_copy(step).wait_recv()
        return total + far_in[step - 1]

    total = lax.fori_loop(1, FAR, add_far, far_out[high])
    lane = lax.broadcasted_iota(jnp.int32, (1, LANES), 1)
    pairs = jnp.sum(jnp.where(lane == low * FAR + high, total[:, LANES:], 0.0), axis=1, keepdims=True)
    out[...] = total[:, :LANES] / jnp.sqrt(jnp.maximum(pairs, 1.0))

    def end_near(step, _):
        near_copy(step).wait_send()
        return 0

    def end_far(step, _):
        far_copy(step).wait_send()
        return 0

    lax.fori_loop(1, NEAR, end_near, 0)
    lax.fori_loop(1, FAR, end_far, 0)
    for copy in across_copies:
        copy.wait_send()

    @pl.when(light)
    def _():
        for copy in beside_copies:
            copy.wait_send()

    @pl.when(core == 1)
    def _():
        two_copy.wait_send()

    @pl.when(jnp.logical_and(core == 1, low == 1))
    def _():
        one_copy.wait_send()


def lag_tables(groups, freqs, lags):
    nfreq = groups * freqs
    shifts = np.arange(lags) - lags // 2
    theta = math.pi * np.mod(np.arange(nfreq)[:, None] * shifts[None, :], 2 * nfreq) / nfreq
    table = np.stack([np.cos(theta), -np.sin(theta)]).reshape(2, groups, freqs, lags)
    table = table.transpose(1, 0, 2, 3).reshape(groups, 2 * freqs, lags)
    return jnp.asarray((table / HALF).astype(np.float32))


def on_device(spectra, pair_bins):
    freqs = spectra.shape[1]
    block = pltpu.VMEM(spectra.shape, BF16)
    square = pltpu.VMEM((CH, CH), F32)
    return pl.pallas_call(
        network_kernel,
        out_shape=jax.ShapeDtypeStruct((1, LANES), F32),
        in_specs=[ANY, ANY, VMEM],
        out_specs=VMEM,
        scratch_shapes=[
            block,
            block,
            block,
            pltpu.VMEM(pair_bins.shape[1:], jnp.int32),
            pltpu.VMEM((3, CH, CH), BF16),
            pltpu.VMEM((2, CH, CH), BF16),
            pltpu.VMEM((CH, CH), BF16),
            pltpu.VMEM((freqs, 2, CH, LANES), BF16),
            pltpu.VMEM((2, freqs, 1, EARLY, LANES), BF16),
            pltpu.VMEM((2, freqs, 2, EARLY, LANES), BF16),
            pltpu.VMEM((CH * (freqs + PAD), LANES), F32),
            pltpu.VMEM((2, 2 * freqs * (CH + PAD), LANES), F32),
            square,
            square,
            pltpu.VMEM((SEGMENTS, 2 * freqs, CLASSES), F32),
            pltpu.VMEM((16, CLASSES), F32),
            pltpu.VMEM((NEAR, FAR + COUNT_ROWS, LANES), F32),
            pltpu.VMEM((NEAR - 1, FAR + COUNT_ROWS, LANES), F32),
            pltpu.VMEM((FAR, 1, 2 * LANES), F32),
            pltpu.VMEM((FAR - 1, 1, 2 * LANES), F32),
            DMA((2,)),
            DMA((7,)),
            DMA((7,)),
            DMA((NEAR - 1,)),
            DMA((NEAR - 1,)),
            DMA((FAR - 1,)),
            DMA((FAR - 1,)),
        ],
        compiler_params=pltpu.CompilerParams(
            collective_id=0, has_side_effects=True, vmem_limit_bytes=60 * 1024 * 1024
        ),
    )(spectra, pair_bins, lag_tables(lax.axis_size("off"), freqs, LANES))


def solution(mesh):
    in_specs = (P("chan", "off", None), P("chan", None, None, None))
    out_specs = P(("chan", "off"), None)
    return jax.shard_map(
        on_device, mesh=mesh, in_specs=in_specs, out_specs=out_specs, check_vma=False
    )
```

```python
import functools
import math

import jax
import jax.numpy as jnp
import numpy as np
from jax import lax
from jax.experimental import pallas as pl
from jax.experimental.pallas import tpu as pltpu
from jax.sharding import PartitionSpec as P

F32 = jnp.float32
BF16 = jnp.bfloat16
MESH = pl.DeviceIdType.MESH
VMEM = pl.BlockSpec(memory_space=pltpu.VMEM)
ANY = pl.BlockSpec(memory_space=pl.ANY)
DMA = pltpu.SemaphoreType.DMA

CH = 256
LANES = 128
EARLY = CH // 2
HALF = LANES // 2
SEGMENTS = 4
CLASSES = 64
PAD = 8
NEAR = 8
FAR = 32
FREQ_UNROLL = 8
STATIC_UNROLL = 64
COUNT_ROWS = 8


def whiten(raw, rows, white, with_rotated):
    channels, freqs, _ = raw.shape
    step = freqs + PAD
    chunk = 32

    def normalise(block, _):
        values = raw[pl.ds(block * chunk, chunk)].astype(F32)
        meansq = jnp.mean(values * values, axis=-1, keepdims=True)
        scaled = values * lax.rsqrt(meansq + 1e-05)
        for channel in range(chunk):
            start = pl.multiple_of((block * chunk + channel) * step, 8)
            rows[pl.ds(start, freqs), :] = scaled[channel]
        return 0

    lax.fori_loop(0, channels // chunk, normalise, 0)

    def regroup(block, _):
        for part in range(FREQ_UNROLL):
            freq = block * FREQ_UNROLL + part
            values = rows[pl.ds(freq, channels, stride=step), :]
            white[freq, 0] = values.astype(BF16)
            if with_rotated:
                lane = lax.broadcasted_iota(jnp.int32, (channels, LANES), 1)
                turned = pltpu.roll(values, HALF, 1)
                white[freq, 1] = jnp.where(lane < HALF, turned, -turned).astype(BF16)
        return 0

    lax.fori_loop(0, freqs // FREQ_UNROLL, regroup, 0)


def cross_pairs(first, second, cross, freqs, top=0):
    step = CH + PAD

    def body(block, _):
        for part in range(FREQ_UNROLL):
            freq = block * FREQ_UNROLL + part
            product = lax.dot_general(
                first(freq), second(freq), (((1,), (1,)), ((), ())), preferred_element_type=F32
            )
            for row in range(2):
                start = pl.multiple_of((top + freq + row * freqs) * step, 8)
                for side in range(product.shape[1] // LANES):
                    cross[side, pl.ds(start, CH), :] = product[
                        row * CH : (row + 1) * CH, side * LANES : (side + 1) * LANES
                    ]
        return 0

    lax.fori_loop(0, freqs // FREQ_UNROLL, body, 0)


def slot_numbers(width, count=CLASSES):
    shape = (count // 16, 16, width)
    ids = lax.broadcasted_iota(jnp.int32, shape, 0) * 16 + lax.broadcasted_iota(jnp.int32, shape, 1)
    return ids.astype(F32).astype(BF16)


def slots_of(marks):
    classes = lax.shift_right_logical(marks, 2)
    return ((classes & 1) * (CLASSES // 2) + lax.shift_right_logical(classes, 1)).astype(F32)


def piece_of(cross, i, nrows, sides):
    pieces = [cross[side, pl.ds(i, nrows, stride=CH + PAD), :] for side in sides]
    return jnp.concatenate(pieces, axis=1).astype(BF16)


def row_of(ref, i, width):
    return jnp.broadcast_to(ref[pl.ds(i, 1), :][:, :width], (16, width)).astype(BF16)


def place_marks(marks, masks, slots, segments):
    width = marks.shape[1]
    groups = SEGMENTS // masks
    segment = marks & (SEGMENTS - 1)
    slots[:, :width] = slots_of(marks) + (CLASSES * (segment & (groups - 1))).astype(F32)
    segments[:, :width] = lax.shift_right_logical(segment, groups // 2).astype(F32)


def add_all_bins(cross, slots, segments, masks, sides, nrows, add_sums, add_tally, begin=0, end=CH):
    width = len(sides) * LANES
    groups = SEGMENTS // masks
    nslots = groups * CLASSES
    slot_ids = slot_numbers(width, nslots)
    unroll = STATIC_UNROLL
    row_ids = lax.broadcasted_iota(jnp.int32, (16, width), 0).astype(F32).astype(BF16)
    one = jnp.ones((), BF16)
    zero = jnp.zeros((), BF16)

    def add_rows(block, _):
        pieces, onehots = [], []
        for part in range(unroll):
            i = block * unroll + part
            values = piece_of(cross, i, nrows, sides).reshape(nrows // 16, 16, width)
            place = row_of(segments, i, width)
            masked = [
                jnp.where(place[None] == jnp.full((), mask, BF16), values, zero).reshape(nrows, width)
                for mask in range(masks)
            ]
            masked.append(jnp.where(place == row_ids, one, zero))
            pieces.append(jnp.concatenate(masked, axis=0))
            row = row_of(slots, i, width)
            onehots.append(jnp.where(row[None] == slot_ids, one, zero).reshape(nslots, width))
        binned = lax.dot_general(
            jnp.concatenate(pieces, axis=1),
            jnp.concatenate(onehots, axis=1),
            (((1,), (1,)), ((), ())),
            preferred_element_type=F32,
        )
        for segment in range(SEGMENTS):
            mask, group = segment // groups, segment % groups
            columns = slice(group * CLASSES, (group + 1) * CLASSES)
            tally_row = masks * nrows + mask
            add_sums(segment, binned[mask * nrows : (mask + 1) * nrows, columns])
            add_tally(segment, binned[tally_row : tally_row + 1, columns])
        return 0

    lax.fori_loop(begin // unroll, end // unroll, add_rows, 0)


def as_integers(values):
    return values.astype(F32).astype(jnp.int32)


def network_kernel(
    spectra, pair_bins, table, out,
    raw, across_raw, beside_raw, labels, sent_labels, across_labels, beside_labels, white, across, beside,
    rows, cross, slots, segments, sums, mate_sums, tally, parts, near_in, far_out, far_in,
    local_sem, send_sem, recv_sem, near_send, near_recv, far_send, far_recv,
):
    freqs = raw.shape[1]
    chan, off = lax.axis_index("chan"), lax.axis_index("off")
    count = lax.axis_size("chan")
    low, high = lax.rem(chan, 2), lax.div(chan, 2)
    core = lax.rem(off, 2)
    heavy = low == core
    light = low != core
    near = off * 2 + low
    target = lax.rem(chan + count - 2 + 4 * core, count)
    partner = chan + 1 - 2 * low
    mate = off + 1 - 2 * core

    def near_device(step):
        index = lax.rem(near + step, NEAR)
        return index, (high * 2 + lax.rem(index, 2), lax.div(index, 2))

    def far_device(step):
        index = lax.rem(high + step, FAR)
        return index, (index * 2 + low, off)

    load_labels = pltpu.make_async_copy(pair_bins.at[0], labels, local_sem.at[0])
    load_raw = pltpu.make_async_copy(spectra, raw, local_sem.at[1])
    load_labels.start()
    load_raw.start()
    barrier = pltpu.get_barrier_semaphore()

    def greet_near(step, _):
        pl.semaphore_signal(barrier, inc=1, device_id=near_device(step)[1], device_id_type=MESH)
        return 0

    def greet_far(step, _):
        pl.semaphore_signal(barrier, inc=1, device_id=far_device(step)[1], device_id_type=MESH)
        return 0

    lax.fori_loop(1, FAR, greet_far, 0)
    lax.fori_loop(1, NEAR, greet_near, 0)
    load_labels.wait()
    one_ahead, two_ahead = labels[1].astype(F32), labels[2].astype(F32)
    one_turned = one_ahead.T
    sent_labels[0] = one_turned.astype(BF16)
    sent_labels[1] = two_ahead.T.astype(BF16)
    sent_labels[2] = jnp.where(core == 0, one_ahead, one_turned).astype(BF16)

    @pl.when(core == 0)
    def _():
        across_labels[0] = one_ahead.astype(BF16)
        across_labels[1] = two_ahead.astype(BF16)

    pl.semaphore_wait(barrier, FAR - 1 + NEAR - 1)

    def remote(index, source, landing, chan_to, off_to=off):
        return pltpu.make_async_remote_copy(
            src_ref=source,
            dst_ref=landing,
            send_sem=send_sem.at[index],
            recv_sem=recv_sem.at[index],
            device_id=(chan_to, off_to),
            device_id_type=MESH,
        )

    pieces = [slice(piece * EARLY, (piece + 1) * EARLY) for piece in range(2)]
    across_copies = [remote(i, spectra.at[part], across_raw.at[part], target) for i, part in enumerate(pieces)]
    beside_copies = [remote(2 + i, spectra.at[part], beside_raw.at[part], partner) for i, part in enumerate(pieces)]
    mate_copies = [remote(7 + i, spectra.at[part], beside_raw.at[part], chan, mate) for i, part in enumerate(pieces)]
    beside_copies.append(remote(4, sent_labels.at[2], beside_labels, partner))
    two_copy = remote(5, sent_labels.at[1], across_labels.at[1], target)
    one_copy = remote(6, sent_labels.at[0], across_labels.at[0], target)
    across_copies[0].start()

    @pl.when(light)
    def _():
        beside_copies[0].start()
        beside_copies[2].start()

    @pl.when(heavy)
    def _():
        for copy in mate_copies:
            copy.start()

    @pl.when(core == 1)
    def _():
        two_copy.start()

    @pl.when(jnp.logical_and(core == 1, low == 1))
    def _():
        one_copy.start()

    place_marks(labels[0], 2, slots, segments)
    sums[...] = jnp.zeros_like(sums)
    mate_sums[...] = jnp.zeros_like(mate_sums)
    tally[...] = jnp.zeros_like(tally)
    load_raw.wait()
    whiten(raw, rows, white, True)

    def own(freq):
        return white[freq].reshape(2 * CH, LANES)

    def add_tally(weight):
        def add(segment, values):
            tally[segment : segment + 1, :] += values * weight

        return add

    def add_self(segment, values):
        sums[segment] += values

    def add_mate(segment, values):
        mate_sums[segment] += values

    counted = (off == 0).astype(F32)
    counted_self = (off < 2).astype(F32)

    sign = (1 - 2 * core).astype(F32)

    def add_pairs(segment, values):
        sums[segment, :freqs] += values[:freqs]
        sums[segment, freqs:] += values[freqs:] * sign

    def bin_pairs(marks):
        place_marks(marks, 2, slots, segments)
        add_all_bins(cross, slots, segments, 2, (0, 1), 2 * freqs, add_pairs, add_tally(counted))

    def whole(block, row):
        return lambda freq: jnp.concatenate([block[0, freq, row], block[1, freq, row]], axis=0)

    def beside_rows(freq):
        return jnp.concatenate([whole(beside, 0)(freq), whole(beside, 1)(freq)], axis=0)

    @pl.when(heavy)
    def _():
        across_copies[0].wait_send()
        across_copies[1].start()

    @pl.when(light)
    def _():
        cross_pairs(own, lambda freq: white[freq, 0], cross, freqs)
        bin_block = functools.partial(add_all_bins, cross, slots, segments, 2, (0, 1), 2 * freqs)
        bin_block(add_self, add_tally(counted_self), begin=0, end=CH // 2)
        across_copies[1].start()
        beside_copies[1].start()
        bin_block(add_self, add_tally(counted_self), begin=CH // 2, end=CH)
        for piece, copy in enumerate(mate_copies):
            copy.wait_recv()
            whiten(beside_raw.at[pieces[piece]], rows, beside.at[piece], True)
        cross_pairs(beside_rows, whole(beside, 0), cross, freqs)
        bin_block(add_mate, add_tally(0.0))

    across_copies[0].wait_recv()
    whiten(across_raw.at[pieces[0]], rows, across.at[0], False)

    @pl.when(core == 1)
    def _():
        two_copy.wait_recv()

    def beside_marks():
        return jnp.where(core == 0, labels[1], as_integers(beside_labels[...]))

    def half_marks(piece):
        lanes = slice(piece * LANES, (piece + 1) * LANES)
        return jnp.concatenate([beside_marks()[:, lanes], as_integers(across_labels[1])[:, lanes]], axis=1)

    def half_blocks(piece):
        return lambda freq: jnp.concatenate([beside[piece, freq, 0], across[piece, freq, 0]], axis=0)

    @pl.when(heavy)
    def _():
        beside_copies[0].wait_recv()
        beside_copies[2].wait_recv()
        whiten(beside_raw.at[pieces[0]], rows, beside.at[0], True)
        cross_pairs(own, half_blocks(0), cross, freqs)
        bin_pairs(half_marks(0))

    across_copies[1].wait_recv()
    whiten(across_raw.at[pieces[1]], rows, across.at[1], False)

    @pl.when(heavy)
    def _():
        beside_copies[1].wait_recv()
        whiten(beside_raw.at[pieces[1]], rows, beside.at[1], True)
        cross_pairs(own, half_blocks(1), cross, freqs)
        bin_pairs(half_marks(1))

        @pl.when(core == 1)
        def _():
            one_copy.wait_recv()

        cross_pairs(beside_rows, whole(across, 0), cross, freqs)
        bin_pairs(as_integers(jnp.where(core == 0, beside_labels[...].astype(F32), across_labels[0].astype(F32))))

    @pl.when(light)
    def _():
        cross_pairs(own, whole(across, 0), cross, freqs)
        bin_pairs(as_integers(across_labels[1]))

    tables = jnp.concatenate([table[off], table[mate]], axis=0)
    for segment in range(SEGMENTS):
        trace = lax.dot_general(
            jnp.concatenate([sums[segment], mate_sums[segment]], axis=0),
            tables,
            (((0,), (0,)), ((), ())),
            precision=lax.Precision.HIGHEST,
            preferred_element_type=F32,
        )
        counts = jnp.broadcast_to(tally[segment : segment + 1, :], (COUNT_ROWS, CLASSES))
        counts = jnp.concatenate([counts, jnp.zeros((COUNT_ROWS, LANES - CLASSES), F32)], axis=1)
        for part in range(2):
            parts[segment * 2 + part, :FAR, :] = trace[part * FAR : (part + 1) * FAR]
            parts[segment * 2 + part, FAR:, :] = counts

    def near_copy(step):
        index, device = near_device(step)
        return pltpu.make_async_remote_copy(
            src_ref=parts.at[index],
            dst_ref=near_in.at[step - 1],
            send_sem=near_send.at[step - 1],
            recv_sem=near_recv.at[step - 1],
            device_id=device,
            device_id_type=MESH,
        )

    def far_copy(step):
        index, device = far_device(step)
        return pltpu.make_async_remote_copy(
            src_ref=far_out.at[index],
            dst_ref=far_in.at[step - 1],
            send_sem=far_send.at[step - 1],
            recv_sem=far_recv.at[step - 1],
            device_id=device,
            device_id_type=MESH,
        )

    def start_near(step, _):
        near_copy(step).start()
        return 0

    def start_far(step, _):
        far_copy(step).start()
        return 0

    lax.fori_loop(1, NEAR, start_near, 0)

    def add_near(step, total):
        near_copy(step).wait_recv()
        return total + near_in[step - 1]

    total = lax.fori_loop(1, NEAR, add_near, parts[near])
    for row in range(FAR):
        far_out[row] = jnp.concatenate([total[row : row + 1], total[FAR : FAR + 1]], axis=1)
    lax.fori_loop(1, FAR, start_far, 0)

    def add_far(step, total):
        far_copy(step).wait_recv()
        return total + far_in[step - 1]

    total = lax.fori_loop(1, FAR, add_far, far_out[high])
    lane = lax.broadcasted_iota(jnp.int32, (1, LANES), 1)
    pairs = jnp.sum(jnp.where(lane == low * FAR + high, total[:, LANES:], 0.0), axis=1, keepdims=True)
    out[...] = total[:, :LANES] / jnp.sqrt(jnp.maximum(pairs, 1.0))

    def end_near(step, _):
        near_copy(step).wait_send()
        return 0

    def end_far(step, _):
        far_copy(step).wait_send()
        return 0

    lax.fori_loop(1, NEAR, end_near, 0)
    lax.fori_loop(1, FAR, end_far, 0)
    across_copies[1].wait_send()

    @pl.when(light)
    def _():
        across_copies[0].wait_send()
        for copy in beside_copies:
            copy.wait_send()

    @pl.when(heavy)
    def _():
        for copy in mate_copies:
            copy.wait_send()

    @pl.when(core == 1)
    def _():
        two_copy.wait_send()

    @pl.when(jnp.logical_and(core == 1, low == 1))
    def _():
        one_copy.wait_send()


def lag_tables(groups, freqs, lags):
    nfreq = groups * freqs
    shifts = np.arange(lags) - lags // 2
    theta = math.pi * np.mod(np.arange(nfreq)[:, None] * shifts[None, :], 2 * nfreq) / nfreq
    table = np.stack([np.cos(theta), -np.sin(theta)]).reshape(2, groups, freqs, lags)
    table = table.transpose(1, 0, 2, 3).reshape(groups, 2 * freqs, lags)
    return jnp.asarray((table / HALF).astype(np.float32))


def on_device(spectra, pair_bins):
    freqs = spectra.shape[1]
    block = pltpu.VMEM(spectra.shape, BF16)
    square = pltpu.VMEM((CH, CH), F32)
    return pl.pallas_call(
        network_kernel,
        out_shape=jax.ShapeDtypeStruct((1, LANES), F32),
        in_specs=[ANY, ANY, VMEM],
        out_specs=VMEM,
        scratch_shapes=[
            block,
            block,
            block,
            pltpu.VMEM(pair_bins.shape[1:], jnp.int32),
            pltpu.VMEM((3, CH, CH), BF16),
            pltpu.VMEM((2, CH, CH), BF16),
            pltpu.VMEM((CH, CH), BF16),
            pltpu.VMEM((freqs, 2, CH, LANES), BF16),
            pltpu.VMEM((2, freqs, 1, EARLY, LANES), BF16),
            pltpu.VMEM((2, freqs, 2, EARLY, LANES), BF16),
            pltpu.VMEM((CH * (freqs + PAD), LANES), F32),
            pltpu.VMEM((2, 2 * freqs * (CH + PAD), LANES), F32),
            square,
            square,
            pltpu.VMEM((SEGMENTS, 2 * freqs, CLASSES), F32),
            pltpu.VMEM((SEGMENTS, 2 * freqs, CLASSES), F32),
            pltpu.VMEM((16, CLASSES), F32),
            pltpu.VMEM((NEAR, FAR + COUNT_ROWS, LANES), F32),
            pltpu.VMEM((NEAR - 1, FAR + COUNT_ROWS, LANES), F32),
            pltpu.VMEM((FAR, 1, 2 * LANES), F32),
            pltpu.VMEM((FAR - 1, 1, 2 * LANES), F32),
            DMA((2,)),
            DMA((9,)),
            DMA((9,)),
            DMA((NEAR - 1,)),
            DMA((NEAR - 1,)),
            DMA((FAR - 1,)),
            DMA((FAR - 1,)),
        ],
        compiler_params=pltpu.CompilerParams(
            collective_id=0, has_side_effects=True, vmem_limit_bytes=60 * 1024 * 1024
        ),
    )(spectra, pair_bins, lag_tables(lax.axis_size("off"), freqs, LANES))


def solution(mesh):
    in_specs = (P("chan", "off", None), P("chan", None, None, None))
    out_specs = P(("chan", "off"), None)
    return jax.shard_map(
        on_device, mesh=mesh, in_specs=in_specs, out_specs=out_specs, check_vma=False
    )
```

```python
import functools
import math

import jax
import jax.numpy as jnp
import numpy as np
from jax import lax
from jax.experimental import pallas as pl
from jax.experimental.pallas import tpu as pltpu
from jax.sharding import PartitionSpec as P

F32 = jnp.float32
BF16 = jnp.bfloat16
MESH = pl.DeviceIdType.MESH
VMEM = pl.BlockSpec(memory_space=pltpu.VMEM)
ANY = pl.BlockSpec(memory_space=pl.ANY)
DMA = pltpu.SemaphoreType.DMA

CH = 256
LANES = 128
EARLY = CH // 2
LATE = CH // 4
HALF = LANES // 2
SEGMENTS = 4
CLASSES = 64
PAD = 8
NEAR = 8
FAR = 32
FREQ_UNROLL = 8
STATIC_UNROLL = 64
COUNT_ROWS = 8


def whiten(raw, rows, white, with_rotated):
    channels, freqs, _ = raw.shape
    step = freqs + PAD
    chunk = 32

    def normalise(block, _):
        values = raw[pl.ds(block * chunk, chunk)].astype(F32)
        meansq = jnp.mean(values * values, axis=-1, keepdims=True)
        scaled = values * lax.rsqrt(meansq + 1e-05)
        for channel in range(chunk):
            start = pl.multiple_of((block * chunk + channel) * step, 8)
            rows[pl.ds(start, freqs), :] = scaled[channel]
        return 0

    lax.fori_loop(0, channels // chunk, normalise, 0)

    def regroup(block, _):
        for part in range(FREQ_UNROLL):
            freq = block * FREQ_UNROLL + part
            values = rows[pl.ds(freq, channels, stride=step), :]
            white[freq, 0] = values.astype(BF16)
            if with_rotated:
                lane = lax.broadcasted_iota(jnp.int32, (channels, LANES), 1)
                turned = pltpu.roll(values, HALF, 1)
                white[freq, 1] = jnp.where(lane < HALF, turned, -turned).astype(BF16)
        return 0

    lax.fori_loop(0, freqs // FREQ_UNROLL, regroup, 0)


def cross_pairs(first, second, cross, freqs, top=0):
    step = CH + PAD

    def body(block, _):
        for part in range(FREQ_UNROLL):
            freq = block * FREQ_UNROLL + part
            product = lax.dot_general(
                first(freq), second(freq), (((1,), (1,)), ((), ())), preferred_element_type=F32
            )
            for row in range(2):
                start = pl.multiple_of((top + freq + row * freqs) * step, 8)
                for side in range(product.shape[1] // LANES):
                    cross[side, pl.ds(start, CH), :] = product[
                        row * CH : (row + 1) * CH, side * LANES : (side + 1) * LANES
                    ]
        return 0

    lax.fori_loop(0, freqs // FREQ_UNROLL, body, 0)


def slot_numbers(width, count=CLASSES):
    shape = (count // 16, 16, width)
    ids = lax.broadcasted_iota(jnp.int32, shape, 0) * 16 + lax.broadcasted_iota(jnp.int32, shape, 1)
    return ids.astype(F32).astype(BF16)


def slots_of(marks):
    classes = lax.shift_right_logical(marks, 2)
    return ((classes & 1) * (CLASSES // 2) + lax.shift_right_logical(classes, 1)).astype(F32)


def piece_of(cross, i, nrows, sides):
    pieces = [cross[side, pl.ds(i, nrows, stride=CH + PAD), :] for side in sides]
    return jnp.concatenate(pieces, axis=1).astype(BF16)


def row_of(ref, i, width):
    return jnp.broadcast_to(ref[pl.ds(i, 1), :][:, :width], (16, width)).astype(BF16)


def place_marks(marks, masks, slots, segments):
    width = marks.shape[1]
    groups = SEGMENTS // masks
    segment = marks & (SEGMENTS - 1)
    slots[:, :width] = slots_of(marks) + (CLASSES * (segment & (groups - 1))).astype(F32)
    segments[:, :width] = lax.shift_right_logical(segment, groups // 2).astype(F32)


def add_all_bins(cross, slots, segments, masks, sides, nrows, add_sums, add_tally, begin=0, end=CH):
    width = len(sides) * LANES
    groups = SEGMENTS // masks
    nslots = groups * CLASSES
    slot_ids = slot_numbers(width, nslots)
    unroll = STATIC_UNROLL
    row_ids = lax.broadcasted_iota(jnp.int32, (16, width), 0).astype(F32).astype(BF16)
    one = jnp.ones((), BF16)
    zero = jnp.zeros((), BF16)

    def add_rows(block, _):
        pieces, onehots = [], []
        for part in range(unroll):
            i = block * unroll + part
            values = piece_of(cross, i, nrows, sides).reshape(nrows // 16, 16, width)
            place = row_of(segments, i, width)
            masked = [
                jnp.where(place[None] == jnp.full((), mask, BF16), values, zero).reshape(nrows, width)
                for mask in range(masks)
            ]
            masked.append(jnp.where(place == row_ids, one, zero))
            pieces.append(jnp.concatenate(masked, axis=0))
            row = row_of(slots, i, width)
            onehots.append(jnp.where(row[None] == slot_ids, one, zero).reshape(nslots, width))
        binned = lax.dot_general(
            jnp.concatenate(pieces, axis=1),
            jnp.concatenate(onehots, axis=1),
            (((1,), (1,)), ((), ())),
            preferred_element_type=F32,
        )
        for segment in range(SEGMENTS):
            mask, group = segment // groups, segment % groups
            columns = slice(group * CLASSES, (group + 1) * CLASSES)
            tally_row = masks * nrows + mask
            add_sums(segment, binned[mask * nrows : (mask + 1) * nrows, columns])
            add_tally(segment, binned[tally_row : tally_row + 1, columns])
        return 0

    lax.fori_loop(begin // unroll, end // unroll, add_rows, 0)


def as_integers(values):
    return values.astype(F32).astype(jnp.int32)


def network_kernel(
    spectra, pair_bins, table, out,
    raw, across_raw, beside_raw, labels, sent_labels, across_labels, beside_labels, white, across, beside,
    rows, cross, slots, segments, sums, mate_sums, tally, parts, near_in, far_out, far_in,
    local_sem, send_sem, recv_sem, near_send, near_recv, far_send, far_recv,
):
    freqs = raw.shape[1]
    chan, off = lax.axis_index("chan"), lax.axis_index("off")
    count = lax.axis_size("chan")
    low, high = lax.rem(chan, 2), lax.div(chan, 2)
    core = lax.rem(off, 2)
    heavy = low == core
    light = low != core
    near = off * 2 + low
    target = lax.rem(chan + count - 2 + 4 * core, count)
    partner = chan + 1 - 2 * low
    mate = off + 1 - 2 * core

    def near_device(step):
        index = lax.rem(near + step, NEAR)
        return index, (high * 2 + lax.rem(index, 2), lax.div(index, 2))

    def far_device(step):
        index = lax.rem(high + step, FAR)
        return index, (index * 2 + low, off)

    load_labels = pltpu.make_async_copy(pair_bins.at[0], labels, local_sem.at[0])
    load_raw = pltpu.make_async_copy(spectra, raw, local_sem.at[1])
    load_labels.start()
    load_raw.start()
    barrier = pltpu.get_barrier_semaphore()

    def greet_near(step, _):
        pl.semaphore_signal(barrier, inc=1, device_id=near_device(step)[1], device_id_type=MESH)
        return 0

    def greet_far(step, _):
        pl.semaphore_signal(barrier, inc=1, device_id=far_device(step)[1], device_id_type=MESH)
        return 0

    lax.fori_loop(1, FAR, greet_far, 0)
    lax.fori_loop(1, NEAR, greet_near, 0)
    load_labels.wait()
    one_ahead, two_ahead = labels[1].astype(F32), labels[2].astype(F32)
    one_turned = one_ahead.T
    sent_labels[0] = one_turned.astype(BF16)
    sent_labels[1] = two_ahead.T.astype(BF16)
    sent_labels[2] = jnp.where(core == 0, one_ahead, one_turned).astype(BF16)

    @pl.when(core == 0)
    def _():
        across_labels[0] = one_ahead.astype(BF16)
        across_labels[1] = two_ahead.astype(BF16)

    pl.semaphore_wait(barrier, FAR - 1 + NEAR - 1)

    def remote(index, source, landing, chan_to, off_to=off):
        return pltpu.make_async_remote_copy(
            src_ref=source,
            dst_ref=landing,
            send_sem=send_sem.at[index],
            recv_sem=recv_sem.at[index],
            device_id=(chan_to, off_to),
            device_id_type=MESH,
        )

    halves = [slice(piece * EARLY, (piece + 1) * EARLY) for piece in range(2)]
    pieces = [slice(0, EARLY), slice(EARLY, EARLY + LATE), slice(EARLY + LATE, CH)]
    across_copies = [remote(i, spectra.at[part], across_raw.at[part], target) for i, part in enumerate(pieces)]
    beside_copies = [remote(3 + i, spectra.at[part], beside_raw.at[part], partner) for i, part in enumerate(pieces)]
    mate_copies = [remote(9 + i, spectra.at[part], beside_raw.at[part], chan, mate) for i, part in enumerate(halves)]
    beside_copies.append(remote(6, sent_labels.at[2], beside_labels, partner))
    two_copy = remote(7, sent_labels.at[1], across_labels.at[1], target)
    one_copy = remote(8, sent_labels.at[0], across_labels.at[0], target)
    across_copies[0].start()

    @pl.when(light)
    def _():
        beside_copies[0].start()
        beside_copies[3].start()

    @pl.when(heavy)
    def _():
        for copy in mate_copies:
            copy.start()

    @pl.when(core == 1)
    def _():
        two_copy.start()

    @pl.when(jnp.logical_and(core == 1, low == 1))
    def _():
        one_copy.start()

    place_marks(labels[0], 2, slots, segments)
    sums[...] = jnp.zeros_like(sums)
    mate_sums[...] = jnp.zeros_like(mate_sums)
    tally[...] = jnp.zeros_like(tally)
    load_raw.wait()
    whiten(raw, rows, white, True)

    def own(freq):
        return white[freq].reshape(2 * CH, LANES)

    def add_tally(weight):
        def add(segment, values):
            tally[segment : segment + 1, :] += values * weight

        return add

    def add_self(segment, values):
        sums[segment] += values

    def add_mate(segment, values):
        mate_sums[segment] += values

    counted = (off == 0).astype(F32)
    counted_self = (off < 2).astype(F32)

    sign = (1 - 2 * core).astype(F32)

    def add_pairs(segment, values):
        sums[segment, :freqs] += values[:freqs]
        sums[segment, freqs:] += values[freqs:] * sign

    def bin_pairs(marks):
        place_marks(marks, 2, slots, segments)
        sides = tuple(range(marks.shape[1] // LANES))
        add_all_bins(cross, slots, segments, 2, sides, 2 * freqs, add_pairs, add_tally(counted))

    def whole(block, row):
        return lambda freq: jnp.concatenate([block[0, freq, row], block[1, freq, row]], axis=0)

    def beside_rows(freq):
        return jnp.concatenate([whole(beside, 0)(freq), whole(beside, 1)(freq)], axis=0)

    @pl.when(heavy)
    def _():
        across_copies[0].wait_send()
        across_copies[1].start()

    @pl.when(light)
    def _():
        cross_pairs(own, lambda freq: white[freq, 0], cross, freqs)
        bin_block = functools.partial(add_all_bins, cross, slots, segments, 2, (0, 1), 2 * freqs)
        bin_block(add_self, add_tally(counted_self))
        across_copies[1].start()
        beside_copies[1].start()
        for piece, copy in enumerate(mate_copies):
            copy.wait_recv()
            whiten(beside_raw.at[halves[piece]], rows, beside.at[piece], True)
        cross_pairs(beside_rows, whole(beside, 0), cross, freqs)
        across_copies[2].start()
        beside_copies[2].start()
        bin_block(add_mate, add_tally(0.0))

    across_copies[0].wait_recv()
    whiten(across_raw.at[pieces[0]], rows, across.at[0], False)

    @pl.when(core == 1)
    def _():
        two_copy.wait_recv()

    def beside_marks():
        return jnp.where(core == 0, labels[1], as_integers(beside_labels[...]))

    def piece_marks(part):
        return jnp.concatenate([beside_marks()[:, part], as_integers(across_labels[1])[:, part]], axis=1)

    def late_part(piece):
        return pl.ds((piece - 1) * LATE, LATE)

    def whiten_across(piece):
        across_copies[piece].wait_recv()
        whiten(across_raw.at[pieces[piece]], rows, across.at[1, :, :, late_part(piece), :], False)

    @pl.when(heavy)
    def _():
        beside_copies[0].wait_recv()
        beside_copies[3].wait_recv()
        whiten(beside_raw.at[pieces[0]], rows, beside.at[0], True)
        cross_pairs(
            own, lambda freq: jnp.concatenate([beside[0, freq, 0], across[0, freq, 0]], axis=0), cross, freqs
        )
        across_copies[2].start()
        bin_pairs(piece_marks(pieces[0]))
        for piece in (1, 2):
            part = late_part(piece)
            whiten_across(piece)
            beside_copies[piece].wait_recv()
            whiten(beside_raw.at[pieces[piece]], rows, beside.at[1, :, :, part, :], True)
            cross_pairs(
                own,
                lambda freq, part=part: jnp.concatenate(
                    [beside[1, freq, 0, part, :], across[1, freq, 0, part, :]], axis=0
                ),
                cross,
                freqs,
            )
            bin_pairs(piece_marks(pieces[piece]))

        @pl.when(core == 1)
        def _():
            one_copy.wait_recv()

        cross_pairs(beside_rows, whole(across, 0), cross, freqs)
        bin_pairs(as_integers(jnp.where(core == 0, beside_labels[...].astype(F32), across_labels[0].astype(F32))))

    @pl.when(light)
    def _():
        whiten_across(1)
        whiten_across(2)
        cross_pairs(own, whole(across, 0), cross, freqs)
        bin_pairs(as_integers(across_labels[1]))

    tables = jnp.concatenate([table[off], table[mate]], axis=0)
    for segment in range(SEGMENTS):
        trace = lax.dot_general(
            jnp.concatenate([sums[segment], mate_sums[segment]], axis=0),
            tables,
            (((0,), (0,)), ((), ())),
            precision=lax.Precision.HIGHEST,
            preferred_element_type=F32,
        )
        counts = jnp.broadcast_to(tally[segment : segment + 1, :], (COUNT_ROWS, CLASSES))
        counts = jnp.concatenate([counts, jnp.zeros((COUNT_ROWS, LANES - CLASSES), F32)], axis=1)
        for part in range(2):
            parts[segment * 2 + part, :FAR, :] = trace[part * FAR : (part + 1) * FAR]
            parts[segment * 2 + part, FAR:, :] = counts

    def near_copy(step):
        index, device = near_device(step)
        return pltpu.make_async_remote_copy(
            src_ref=parts.at[index],
            dst_ref=near_in.at[step - 1],
            send_sem=near_send.at[step - 1],
            recv_sem=near_recv.at[step - 1],
            device_id=device,
            device_id_type=MESH,
        )

    def far_copy(step):
        index, device = far_device(step)
        return pltpu.make_async_remote_copy(
            src_ref=far_out.at[index],
            dst_ref=far_in.at[step - 1],
            send_sem=far_send.at[step - 1],
            recv_sem=far_recv.at[step - 1],
            device_id=device,
            device_id_type=MESH,
        )

    def start_near(step, _):
        near_copy(step).start()
        return 0

    def start_far(step, _):
        far_copy(step).start()
        return 0

    lax.fori_loop(1, NEAR, start_near, 0)

    def add_near(step, total):
        near_copy(step).wait_recv()
        return total + near_in[step - 1]

    total = lax.fori_loop(1, NEAR, add_near, parts[near])
    for row in range(FAR):
        far_out[row] = jnp.concatenate([total[row : row + 1], total[FAR : FAR + 1]], axis=1)
    lax.fori_loop(1, FAR, start_far, 0)

    def add_far(step, total):
        far_copy(step).wait_recv()
        return total + far_in[step - 1]

    total = lax.fori_loop(1, FAR, add_far, far_out[high])
    lane = lax.broadcasted_iota(jnp.int32, (1, LANES), 1)
    pairs = jnp.sum(jnp.where(lane == low * FAR + high, total[:, LANES:], 0.0), axis=1, keepdims=True)
    out[...] = total[:, :LANES] / jnp.sqrt(jnp.maximum(pairs, 1.0))

    def end_near(step, _):
        near_copy(step).wait_send()
        return 0

    def end_far(step, _):
        far_copy(step).wait_send()
        return 0

    lax.fori_loop(1, NEAR, end_near, 0)
    lax.fori_loop(1, FAR, end_far, 0)
    across_copies[1].wait_send()
    across_copies[2].wait_send()

    @pl.when(light)
    def _():
        across_copies[0].wait_send()
        for copy in beside_copies:
            copy.wait_send()

    @pl.when(heavy)
    def _():
        for copy in mate_copies:
            copy.wait_send()

    @pl.when(core == 1)
    def _():
        two_copy.wait_send()

    @pl.when(jnp.logical_and(core == 1, low == 1))
    def _():
        one_copy.wait_send()


def lag_tables(groups, freqs, lags):
    nfreq = groups * freqs
    shifts = np.arange(lags) - lags // 2
    theta = math.pi * np.mod(np.arange(nfreq)[:, None] * shifts[None, :], 2 * nfreq) / nfreq
    table = np.stack([np.cos(theta), -np.sin(theta)]).reshape(2, groups, freqs, lags)
    table = table.transpose(1, 0, 2, 3).reshape(groups, 2 * freqs, lags)
    return jnp.asarray((table / HALF).astype(np.float32))


def on_device(spectra, pair_bins):
    freqs = spectra.shape[1]
    block = pltpu.VMEM(spectra.shape, BF16)
    square = pltpu.VMEM((CH, CH), F32)
    return pl.pallas_call(
        network_kernel,
        out_shape=jax.ShapeDtypeStruct((1, LANES), F32),
        in_specs=[ANY, ANY, VMEM],
        out_specs=VMEM,
        scratch_shapes=[
            block,
            block,
            block,
            pltpu.VMEM(pair_bins.shape[1:], jnp.int32),
            pltpu.VMEM((3, CH, CH), BF16),
            pltpu.VMEM((2, CH, CH), BF16),
            pltpu.VMEM((CH, CH), BF16),
            pltpu.VMEM((freqs, 2, CH, LANES), BF16),
            pltpu.VMEM((2, freqs, 1, EARLY, LANES), BF16),
            pltpu.VMEM((2, freqs, 2, EARLY, LANES), BF16),
            pltpu.VMEM((CH * (freqs + PAD), LANES), F32),
            pltpu.VMEM((2, 2 * freqs * (CH + PAD), LANES), F32),
            square,
            square,
            pltpu.VMEM((SEGMENTS, 2 * freqs, CLASSES), F32),
            pltpu.VMEM((SEGMENTS, 2 * freqs, CLASSES), F32),
            pltpu.VMEM((16, CLASSES), F32),
            pltpu.VMEM((NEAR, FAR + COUNT_ROWS, LANES), F32),
            pltpu.VMEM((NEAR - 1, FAR + COUNT_ROWS, LANES), F32),
            pltpu.VMEM((FAR, 1, 2 * LANES), F32),
            pltpu.VMEM((FAR - 1, 1, 2 * LANES), F32),
            DMA((2,)),
            DMA((11,)),
            DMA((11,)),
            DMA((NEAR - 1,)),
            DMA((NEAR - 1,)),
            DMA((FAR - 1,)),
            DMA((FAR - 1,)),
        ],
        compiler_params=pltpu.CompilerParams(
            collective_id=0, has_side_effects=True, vmem_limit_bytes=60 * 1024 * 1024
        ),
    )(spectra, pair_bins, lag_tables(lax.axis_size("off"), freqs, LANES))


def solution(mesh):
    in_specs = (P("chan", "off", None), P("chan", None, None, None))
    out_specs = P(("chan", "off"), None)
    return jax.shard_map(
        on_device, mesh=mesh, in_specs=in_specs, out_specs=out_specs, check_vma=False
    )
```

```python
import functools
import math

import jax
import jax.numpy as jnp
import numpy as np
from jax import lax
from jax.experimental import pallas as pl
from jax.experimental.pallas import tpu as pltpu
from jax.sharding import PartitionSpec as P

F32 = jnp.float32
BF16 = jnp.bfloat16
MESH = pl.DeviceIdType.MESH
VMEM = pl.BlockSpec(memory_space=pltpu.VMEM)
ANY = pl.BlockSpec(memory_space=pl.ANY)
DMA = pltpu.SemaphoreType.DMA

CH = 256
LANES = 128
EARLY = CH // 2
LATE = CH // 4
HALF = LANES // 2
SEGMENTS = 4
CLASSES = 64
PAD = 8
NEAR = 8
FAR = 32
FREQ_UNROLL = 8
STATIC_UNROLL = 64
COUNT_ROWS = 8


def whiten(raw, rows, white, with_rotated):
    channels, freqs, _ = raw.shape
    step = freqs + PAD
    chunk = 32

    def normalise(block, _):
        values = raw[pl.ds(block * chunk, chunk)].astype(F32)
        meansq = jnp.mean(values * values, axis=-1, keepdims=True)
        scaled = values * lax.rsqrt(meansq + 1e-05)
        for channel in range(chunk):
            start = pl.multiple_of((block * chunk + channel) * step, 8)
            rows[pl.ds(start, freqs), :] = scaled[channel]
        return 0

    lax.fori_loop(0, channels // chunk, normalise, 0)

    def regroup(block, _):
        for part in range(FREQ_UNROLL):
            freq = block * FREQ_UNROLL + part
            values = rows[pl.ds(freq, channels, stride=step), :]
            white[freq, 0] = values.astype(BF16)
            if with_rotated:
                lane = lax.broadcasted_iota(jnp.int32, (channels, LANES), 1)
                turned = pltpu.roll(values, HALF, 1)
                white[freq, 1] = jnp.where(lane < HALF, turned, -turned).astype(BF16)
        return 0

    lax.fori_loop(0, freqs // FREQ_UNROLL, regroup, 0)


def cross_pairs(first, second, cross, freqs, top=0):
    step = CH + PAD

    def body(block, _):
        for part in range(FREQ_UNROLL):
            freq = block * FREQ_UNROLL + part
            product = lax.dot_general(
                first(freq), second(freq), (((1,), (1,)), ((), ())), preferred_element_type=F32
            )
            for row in range(2):
                start = pl.multiple_of((top + freq + row * freqs) * step, 8)
                for side in range(product.shape[1] // LANES):
                    cross[side, pl.ds(start, CH), :] = product[
                        row * CH : (row + 1) * CH, side * LANES : (side + 1) * LANES
                    ]
        return 0

    lax.fori_loop(0, freqs // FREQ_UNROLL, body, 0)


def slot_numbers(width, count=CLASSES):
    shape = (count // 16, 16, width)
    ids = lax.broadcasted_iota(jnp.int32, shape, 0) * 16 + lax.broadcasted_iota(jnp.int32, shape, 1)
    return ids.astype(F32).astype(BF16)


def slots_of(marks):
    classes = lax.shift_right_logical(marks, 2)
    return ((classes & 1) * (CLASSES // 2) + lax.shift_right_logical(classes, 1)).astype(F32)


def piece_of(cross, i, nrows, sides):
    pieces = [cross[side, pl.ds(i, nrows, stride=CH + PAD), :] for side in sides]
    return jnp.concatenate(pieces, axis=1).astype(BF16)


def row_of(ref, i, width):
    return jnp.broadcast_to(ref[pl.ds(i, 1), :][:, :width], (16, width)).astype(BF16)


def place_marks(marks, masks, slots, segments):
    width = marks.shape[1]
    groups = SEGMENTS // masks
    segment = marks & (SEGMENTS - 1)
    slots[:, :width] = slots_of(marks) + (CLASSES * (segment & (groups - 1))).astype(F32)
    segments[:, :width] = lax.shift_right_logical(segment, groups // 2).astype(F32)


def add_all_bins(cross, slots, segments, masks, sides, nrows, add_sums, add_tally, begin=0, end=CH):
    width = len(sides) * LANES
    groups = SEGMENTS // masks
    nslots = groups * CLASSES
    slot_ids = slot_numbers(width, nslots)
    unroll = STATIC_UNROLL
    row_ids = lax.broadcasted_iota(jnp.int32, (16, width), 0).astype(F32).astype(BF16)
    one = jnp.ones((), BF16)
    zero = jnp.zeros((), BF16)

    def add_rows(block, _):
        pieces, onehots = [], []
        for part in range(unroll):
            i = block * unroll + part
            values = piece_of(cross, i, nrows, sides).reshape(nrows // 16, 16, width)
            place = row_of(segments, i, width)
            masked = [
                jnp.where(place[None] == jnp.full((), mask, BF16), values, zero).reshape(nrows, width)
                for mask in range(masks)
            ]
            masked.append(jnp.where(place == row_ids, one, zero))
            pieces.append(jnp.concatenate(masked, axis=0))
            row = row_of(slots, i, width)
            onehots.append(jnp.where(row[None] == slot_ids, one, zero).reshape(nslots, width))
        binned = lax.dot_general(
            jnp.concatenate(pieces, axis=1),
            jnp.concatenate(onehots, axis=1),
            (((1,), (1,)), ((), ())),
            preferred_element_type=F32,
        )
        for segment in range(SEGMENTS):
            mask, group = segment // groups, segment % groups
            columns = slice(group * CLASSES, (group + 1) * CLASSES)
            tally_row = masks * nrows + mask
            add_sums(segment, binned[mask * nrows : (mask + 1) * nrows, columns])
            add_tally(segment, binned[tally_row : tally_row + 1, columns])
        return 0

    lax.fori_loop(begin // unroll, end // unroll, add_rows, 0)


def as_integers(values):
    return values.astype(F32).astype(jnp.int32)


def network_kernel(
    spectra, pair_bins, table, out,
    raw, across_raw, beside_raw, labels, sent_labels, across_labels, beside_labels, white, across, beside,
    rows, cross, slots, segments, sums, mate_sums, tally, parts, near_in, far_out, far_in,
    local_sem, send_sem, recv_sem, near_send, near_recv, far_send, far_recv,
):
    freqs = raw.shape[1]
    chan, off = lax.axis_index("chan"), lax.axis_index("off")
    count = lax.axis_size("chan")
    low, high = lax.rem(chan, 2), lax.div(chan, 2)
    core = lax.rem(off, 2)
    heavy = low == core
    light = low != core
    near = off * 2 + low
    target = lax.rem(chan + count - 2 + 4 * core, count)
    partner = chan + 1 - 2 * low
    mate = off + 1 - 2 * core

    def near_device(step):
        index = lax.rem(near + step, NEAR)
        return index, (high * 2 + lax.rem(index, 2), lax.div(index, 2))

    def far_device(step):
        index = lax.rem(high + step, FAR)
        return index, (index * 2 + low, off)

    load_labels = pltpu.make_async_copy(pair_bins.at[0], labels, local_sem.at[0])
    load_raw = pltpu.make_async_copy(spectra, raw, local_sem.at[1])
    load_labels.start()
    load_raw.start()
    barrier = pltpu.get_barrier_semaphore()

    def greet_near(step, _):
        pl.semaphore_signal(barrier, inc=1, device_id=near_device(step)[1], device_id_type=MESH)
        return 0

    def greet_far(step, _):
        pl.semaphore_signal(barrier, inc=1, device_id=far_device(step)[1], device_id_type=MESH)
        return 0

    lax.fori_loop(1, FAR, greet_far, 0)
    lax.fori_loop(1, NEAR, greet_near, 0)
    load_labels.wait()
    one_ahead, two_ahead = labels[1].astype(F32), labels[2].astype(F32)
    one_turned = one_ahead.T
    sent_labels[0] = one_turned.astype(BF16)
    sent_labels[1] = two_ahead.T.astype(BF16)
    sent_labels[2] = jnp.where(core == 0, one_ahead, one_turned).astype(BF16)

    @pl.when(core == 0)
    def _():
        across_labels[0] = one_ahead.astype(BF16)
        across_labels[1] = two_ahead.astype(BF16)

    pl.semaphore_wait(barrier, FAR - 1 + NEAR - 1)

    def remote(index, source, landing, chan_to, off_to=off):
        return pltpu.make_async_remote_copy(
            src_ref=source,
            dst_ref=landing,
            send_sem=send_sem.at[index],
            recv_sem=recv_sem.at[index],
            device_id=(chan_to, off_to),
            device_id_type=MESH,
        )

    halves = [slice(piece * EARLY, (piece + 1) * EARLY) for piece in range(2)]
    pieces = [slice(piece * LATE, (piece + 1) * LATE) for piece in range(4)]
    across_copies = [remote(i, spectra.at[part], across_raw.at[part], target) for i, part in enumerate(pieces)]
    beside_copies = [remote(4 + i, spectra.at[part], beside_raw.at[part], partner) for i, part in enumerate(pieces)]
    mate_copies = [remote(11 + i, spectra.at[part], beside_raw.at[part], chan, mate) for i, part in enumerate(halves)]
    beside_copies.append(remote(8, sent_labels.at[2], beside_labels, partner))
    two_copy = remote(9, sent_labels.at[1], across_labels.at[1], target)
    one_copy = remote(10, sent_labels.at[0], across_labels.at[0], target)
    across_copies[0].start()

    @pl.when(light)
    def _():
        beside_copies[0].start()
        beside_copies[4].start()

    @pl.when(heavy)
    def _():
        for copy in mate_copies:
            copy.start()

    @pl.when(core == 1)
    def _():
        two_copy.start()

    @pl.when(jnp.logical_and(core == 1, low == 1))
    def _():
        one_copy.start()

    place_marks(labels[0], 2, slots, segments)
    sums[...] = jnp.zeros_like(sums)
    mate_sums[...] = jnp.zeros_like(mate_sums)
    tally[...] = jnp.zeros_like(tally)
    load_raw.wait()
    whiten(raw, rows, white, True)

    def own(freq):
        return white[freq].reshape(2 * CH, LANES)

    def add_tally(weight):
        def add(segment, values):
            tally[segment : segment + 1, :] += values * weight

        return add

    def add_self(segment, values):
        sums[segment] += values

    def add_mate(segment, values):
        mate_sums[segment] += values

    counted = (off == 0).astype(F32)
    counted_self = (off < 2).astype(F32)

    sign = (1 - 2 * core).astype(F32)

    def add_pairs(segment, values):
        sums[segment, :freqs] += values[:freqs]
        sums[segment, freqs:] += values[freqs:] * sign

    def bin_pairs(marks):
        place_marks(marks, 2, slots, segments)
        sides = tuple(range(marks.shape[1] // LANES))
        add_all_bins(cross, slots, segments, 2, sides, 2 * freqs, add_pairs, add_tally(counted))

    def whole(block, row):
        return lambda freq: jnp.concatenate([block[0, freq, row], block[1, freq, row]], axis=0)

    def beside_rows(freq):
        return jnp.concatenate([whole(beside, 0)(freq), whole(beside, 1)(freq)], axis=0)

    @pl.when(heavy)
    def _():
        across_copies[1].start()
        across_copies[0].wait_send()
        across_copies[2].start()

    @pl.when(light)
    def _():
        across_copies[1].start()
        beside_copies[1].start()
        cross_pairs(own, lambda freq: white[freq, 0], cross, freqs)
        bin_block = functools.partial(add_all_bins, cross, slots, segments, 2, (0, 1), 2 * freqs)
        bin_block(add_self, add_tally(counted_self), begin=0, end=CH // 2)
        across_copies[2].start()
        beside_copies[2].start()
        bin_block(add_self, add_tally(counted_self), begin=CH // 2, end=CH)
        across_copies[3].start()
        beside_copies[3].start()
        for piece, copy in enumerate(mate_copies):
            copy.wait_recv()
            whiten(beside_raw.at[halves[piece]], rows, beside.at[piece], True)
        cross_pairs(beside_rows, whole(beside, 0), cross, freqs)
        bin_block(add_mate, add_tally(0.0))

    @pl.when(core == 1)
    def _():
        two_copy.wait_recv()

    def beside_marks():
        return jnp.where(core == 0, labels[1], as_integers(beside_labels[...]))

    def piece_marks(part):
        return jnp.concatenate([beside_marks()[:, part], as_integers(across_labels[1])[:, part]], axis=1)

    def place_of(piece):
        return piece // 2, pl.ds(piece % 2 * LATE, LATE)

    def whiten_across(piece):
        side, part = place_of(piece)
        across_copies[piece].wait_recv()
        whiten(across_raw.at[pieces[piece]], rows, across.at[side, :, :, part, :], False)

    @pl.when(heavy)
    def _():
        beside_copies[4].wait_recv()
        for piece in range(4):
            side, part = place_of(piece)
            whiten_across(piece)
            beside_copies[piece].wait_recv()
            whiten(beside_raw.at[pieces[piece]], rows, beside.at[side, :, :, part, :], True)
            cross_pairs(
                own,
                lambda freq, side=side, part=part: jnp.concatenate(
                    [beside[side, freq, 0, part, :], across[side, freq, 0, part, :]], axis=0
                ),
                cross,
                freqs,
            )
            if piece == 0:
                across_copies[3].start()
            bin_pairs(piece_marks(pieces[piece]))

        @pl.when(core == 1)
        def _():
            one_copy.wait_recv()

        cross_pairs(beside_rows, whole(across, 0), cross, freqs)
        bin_pairs(as_integers(jnp.where(core == 0, beside_labels[...].astype(F32), across_labels[0].astype(F32))))

    @pl.when(light)
    def _():
        for piece in range(4):
            whiten_across(piece)
        cross_pairs(own, whole(across, 0), cross, freqs)
        bin_pairs(as_integers(across_labels[1]))

    tables = jnp.concatenate([table[off], table[mate]], axis=0)
    for segment in range(SEGMENTS):
        trace = lax.dot_general(
            jnp.concatenate([sums[segment], mate_sums[segment]], axis=0),
            tables,
            (((0,), (0,)), ((), ())),
            precision=lax.Precision.HIGHEST,
            preferred_element_type=F32,
        )
        counts = jnp.broadcast_to(tally[segment : segment + 1, :], (COUNT_ROWS, CLASSES))
        counts = jnp.concatenate([counts, jnp.zeros((COUNT_ROWS, LANES - CLASSES), F32)], axis=1)
        for part in range(2):
            parts[segment * 2 + part, :FAR, :] = trace[part * FAR : (part + 1) * FAR]
            parts[segment * 2 + part, FAR:, :] = counts

    def near_copy(step):
        index, device = near_device(step)
        return pltpu.make_async_remote_copy(
            src_ref=parts.at[index],
            dst_ref=near_in.at[step - 1],
            send_sem=near_send.at[step - 1],
            recv_sem=near_recv.at[step - 1],
            device_id=device,
            device_id_type=MESH,
        )

    def far_copy(step):
        index, device = far_device(step)
        return pltpu.make_async_remote_copy(
            src_ref=far_out.at[index],
            dst_ref=far_in.at[step - 1],
            send_sem=far_send.at[step - 1],
            recv_sem=far_recv.at[step - 1],
            device_id=device,
            device_id_type=MESH,
        )

    def start_near(step, _):
        near_copy(step).start()
        return 0

    def start_far(step, _):
        far_copy(step).start()
        return 0

    lax.fori_loop(1, NEAR, start_near, 0)

    def add_near(step, total):
        near_copy(step).wait_recv()
        return total + near_in[step - 1]

    total = lax.fori_loop(1, NEAR, add_near, parts[near])
    for row in range(FAR):
        far_out[row] = jnp.concatenate([total[row : row + 1], total[FAR : FAR + 1]], axis=1)
    lax.fori_loop(1, FAR, start_far, 0)

    def add_far(step, total):
        far_copy(step).wait_recv()
        return total + far_in[step - 1]

    total = lax.fori_loop(1, FAR, add_far, far_out[high])
    lane = lax.broadcasted_iota(jnp.int32, (1, LANES), 1)
    pairs = jnp.sum(jnp.where(lane == low * FAR + high, total[:, LANES:], 0.0), axis=1, keepdims=True)
    out[...] = total[:, :LANES] / jnp.sqrt(jnp.maximum(pairs, 1.0))

    def end_near(step, _):
        near_copy(step).wait_send()
        return 0

    def end_far(step, _):
        far_copy(step).wait_send()
        return 0

    lax.fori_loop(1, NEAR, end_near, 0)
    lax.fori_loop(1, FAR, end_far, 0)
    across_copies[1].wait_send()
    across_copies[2].wait_send()
    across_copies[3].wait_send()

    @pl.when(light)
    def _():
        across_copies[0].wait_send()
        for copy in beside_copies:
            copy.wait_send()

    @pl.when(heavy)
    def _():
        for copy in mate_copies:
            copy.wait_send()

    @pl.when(core == 1)
    def _():
        two_copy.wait_send()

    @pl.when(jnp.logical_and(core == 1, low == 1))
    def _():
        one_copy.wait_send()


def lag_tables(groups, freqs, lags):
    nfreq = groups * freqs
    shifts = np.arange(lags) - lags // 2
    theta = math.pi * np.mod(np.arange(nfreq)[:, None] * shifts[None, :], 2 * nfreq) / nfreq
    table = np.stack([np.cos(theta), -np.sin(theta)]).reshape(2, groups, freqs, lags)
    table = table.transpose(1, 0, 2, 3).reshape(groups, 2 * freqs, lags)
    return jnp.asarray((table / HALF).astype(np.float32))


def on_device(spectra, pair_bins):
    freqs = spectra.shape[1]
    block = pltpu.VMEM(spectra.shape, BF16)
    square = pltpu.VMEM((CH, CH), F32)
    return pl.pallas_call(
        network_kernel,
        out_shape=jax.ShapeDtypeStruct((1, LANES), F32),
        in_specs=[ANY, ANY, VMEM],
        out_specs=VMEM,
        scratch_shapes=[
            block,
            block,
            block,
            pltpu.VMEM(pair_bins.shape[1:], jnp.int32),
            pltpu.VMEM((3, CH, CH), BF16),
            pltpu.VMEM((2, CH, CH), BF16),
            pltpu.VMEM((CH, CH), BF16),
            pltpu.VMEM((freqs, 2, CH, LANES), BF16),
            pltpu.VMEM((2, freqs, 1, EARLY, LANES), BF16),
            pltpu.VMEM((2, freqs, 2, EARLY, LANES), BF16),
            pltpu.VMEM((CH * (freqs + PAD), LANES), F32),
            pltpu.VMEM((2, 2 * freqs * (CH + PAD), LANES), F32),
            square,
            square,
            pltpu.VMEM((SEGMENTS, 2 * freqs, CLASSES), F32),
            pltpu.VMEM((SEGMENTS, 2 * freqs, CLASSES), F32),
            pltpu.VMEM((16, CLASSES), F32),
            pltpu.VMEM((NEAR, FAR + COUNT_ROWS, LANES), F32),
            pltpu.VMEM((NEAR - 1, FAR + COUNT_ROWS, LANES), F32),
            pltpu.VMEM((FAR, 1, 2 * LANES), F32),
            pltpu.VMEM((FAR - 1, 1, 2 * LANES), F32),
            DMA((2,)),
            DMA((13,)),
            DMA((13,)),
            DMA((NEAR - 1,)),
            DMA((NEAR - 1,)),
            DMA((FAR - 1,)),
            DMA((FAR - 1,)),
        ],
        compiler_params=pltpu.CompilerParams(
            collective_id=0, has_side_effects=True, vmem_limit_bytes=60 * 1024 * 1024
        ),
    )(spectra, pair_bins, lag_tables(lax.axis_size("off"), freqs, LANES))


def solution(mesh):
    in_specs = (P("chan", "off", None), P("chan", None, None, None))
    out_specs = P(("chan", "off"), None)
    return jax.shard_map(
        on_device, mesh=mesh, in_specs=in_specs, out_specs=out_specs, check_vma=False
    )
```
